32 devices in a mesh: dp: 2 (over y), ulysses: 4 (over x, core), blk: 4 (over z).
Axes of the slice: x: 2, y: 2, z: 4, core: 2. Of those that a mesh axis runs over, the one named last changes fastest.
Arguments:
- hidden_in: bfloat16 [2, 2048, 4096], P('dp', ('blk', 'ulysses')), may hold values from -6 to 6
- queries: bfloat16 [2, 2048, 2048], P('dp', ('blk', 'ulysses')), may hold values from -240 to 240
- pair_weight: bfloat16 [4096, 2048], P(('dp', 'blk')), may hold values from -0.09375 to 0.09375
- span_order: int32 [2, 8], P('dp'), may hold values from 0 to 7, each once within a row
- yarn_divisor: int32 [64], replicated, may hold values from 1 to 8
Outputs:
- attended: bfloat16 [2, 2048, 2048], P('dp', ('blk', 'ulysses'))
The draws below stay inside these ranges and needn't reach their ends.
All inputs are finite; a program needn't handle non-finite values.
Results may differ from the reference program's by a relative error of at most 0.02.
The reference program's roundings to bfloat16 on the way count: a program that leaves them out, or rounds other values in their place, can miss the bound.
Values may be sent and summed in bfloat16 or wider, within the bound.
No kernel may reach another device: no remote copies, remote signals or barrier semaphores. Data moves between devices by JAX's collectives and lax.ppermute only.
A program may use at most 128 MiB of HBM per device.

```python
import math
import jax
import jax.numpy as jnp
from jax import lax

D = 4096
KVH = 8
HD = 128
QH = 16
STEPS = 3
SEQS = 2
BLOCKS = 4
BLOCK = 512
SPAN = 256
SEQ = 2048


def draw_queries(key, part):
    first_key, second_key, third_key = jax.random.split(key, 3)
    shape_full = (SEQS, SEQ, QH, HD)
    base_values = jnp.clip(jax.random.normal(first_key, shape_full, jnp.float32), -4.0, 4.0)
    picked = jax.random.randint(second_key, (SEQS, SEQ, QH, 1), 0, 64) == 0
    boost = jnp.exp(jax.random.uniform(third_key, (SEQS, SEQ, QH, 1), jnp.float32, math.log(30.0), math.log(60.0)))
    scaled = base_values * jnp.where(picked, boost, 1.0)
    return scaled.reshape(SEQS, SEQ, QH * HD).astype(jnp.bfloat16)


def with_ends(entries, rng, low, top_value):
    place = [jax.random.randint(jax.random.fold_in(rng, axis), (), 0, length) for axis, length in enumerate(entries.shape)]
    longest = entries.shape.index(max(entries.shape))
    neighbour = place[:longest] + [(place[longest] + 1) % entries.shape[longest]] + place[longest + 1:]
    return entries.at[tuple(place)].set(low).at[tuple(neighbour)].set(top_value)


def block_levels(stream_key, extent, pieces, least, high):
    level = 1.0
    for dim, shards_of in pieces:
        heights = jax.random.uniform(jax.random.fold_in(jax.random.fold_in(stream_key, 6), dim), (shards_of,), jnp.float32, least / len(pieces), high / len(pieces))
        level = level * jnp.repeat(jnp.exp(heights), extent[dim] // shards_of).reshape((-1,) + (1,) * (len(extent) - 1 - dim))
    return level


def scatter_about(own_key, dims, width, bound, cuts=(), kind=jnp.bfloat16):
    entries = width * jax.random.normal(own_key, dims, jnp.float32)
    if cuts:
        entries = entries * block_levels(own_key, dims, cuts, -0.22, 0.18)
    return jnp.clip(entries, -bound, bound).astype(kind)


def setup_inputs(seed: int = 0) -> dict:
    arg_keys = jax.random.split(jax.random.key(seed), 6)
    hidden_in = scatter_about(arg_keys[0], (SEQS, SEQ, D), 1.0, 6.0, ((0, 2), (1, 16)))
    queries = draw_queries(jax.random.fold_in(arg_keys[5], 71), 0)
    pair_weight = scatter_about(arg_keys[2], (D, 2 * KVH * HD), D ** -0.5, 0.09375, ((0, 8),))
    span_order = jax.vmap(lambda own: jax.random.permutation(own, 2 * BLOCKS))(jax.random.split(arg_keys[3], SEQS)).reshape((SEQS, 2 * BLOCKS)).astype(jnp.int32)
    yarn_divisor = with_ends(jax.random.randint(arg_keys[4], (HD // 2,), 1, 9), jax.random.fold_in(arg_keys[4], 1), 1, 8).astype(jnp.int32)
    return dict(hidden_in=hidden_in, queries=queries, pair_weight=pair_weight, span_order=span_order, yarn_divisor=yarn_divisor)


LOG_BASE = math.log(500000.0)

def rotate(vectors, angle_table):
    half_dim = vectors.shape[-1] // 2
    first_half = vectors[..., :half_dim]
    second_half = vectors[..., half_dim:]
    cosine = jnp.cos(angle_table)
    sine_part = jnp.sin(angle_table)
    return jnp.concatenate([first_half * cosine - second_half * sine_part, second_half * cosine + first_half * sine_part], axis=-1)

def angles(positions, yarn_divisor):
    half_dim = yarn_divisor.shape[0]
    scaled = 2.0 * jnp.arange(half_dim, dtype=jnp.float32) / (2 * half_dim)
    inverse = jnp.exp(-LOG_BASE * scaled) / yarn_divisor.astype(jnp.float32)
    return positions.astype(jnp.float32)[:, None] * inverse[None, :]

def reference(hidden_in, queries, pair_weight, span_order, yarn_divisor):
    score_scale = 1.0 / math.sqrt(HD)
    group_size = QH // KVH
    kv_width = KVH * HD
    rows_all = jnp.arange(SEQ, dtype=jnp.int32)
    results = []
    for sequence in range(SEQS):
        positions = (span_order[sequence][rows_all // SPAN] * SPAN + rows_all % SPAN).astype(jnp.int32)
        angle_table = angles(positions, yarn_divisor)[:, None, :]
        projected = jnp.dot(hidden_in[sequence], pair_weight, preferred_element_type=jnp.float32)
        keys = rotate(projected[:, :kv_width].reshape(SEQ, KVH, HD), angle_table).astype(jnp.bfloat16)
        values = projected[:, kv_width:].astype(jnp.bfloat16).reshape(SEQ, KVH, HD)
        rotated = rotate(queries[sequence].astype(jnp.float32).reshape(SEQ, QH, HD), angle_table).astype(jnp.bfloat16)
        keys_by_head = keys.transpose(1, 0, 2)
        values_by_head = values.transpose(1, 0, 2)

        def one_head(flat_index):
            block_index = (flat_index // QH).astype(jnp.int32)
            head_index = (flat_index % QH).astype(jnp.int32)
            kv_head = (head_index // group_size).astype(jnp.int32)
            row_start = (block_index * BLOCK).astype(jnp.int32)
            query_rows = lax.dynamic_slice(rotated, (row_start, head_index, jnp.int32(0)), (BLOCK, 1, HD))[:, 0, :]
            query_pos = lax.dynamic_slice(positions, (row_start,), (BLOCK,))
            source_blocks = (block_index - jnp.arange(STEPS + 1, dtype=jnp.int32)) % BLOCKS
            key_index = (source_blocks[:, None] * BLOCK + jnp.arange(BLOCK, dtype=jnp.int32)[None, :]).reshape(-1).astype(jnp.int32)
            key_rows = lax.dynamic_index_in_dim(keys_by_head, kv_head, 0, False)[key_index]
            value_rows = lax.dynamic_index_in_dim(values_by_head, kv_head, 0, False)[key_index]
            key_pos = positions[key_index]
            score = jnp.dot(query_rows, key_rows.T, preferred_element_type=jnp.float32) * score_scale
            allowed = key_pos[None, :] <= query_pos[:, None]
            row_top = lax.optimization_barrier(jnp.max(jnp.where(allowed, score, -jnp.inf), axis=1))
            weights = jnp.where(allowed, jnp.exp(score - row_top[:, None]), 0.0)
            denominator = lax.optimization_barrier(jnp.sum(weights, axis=1))
            numerator = jnp.dot(weights.astype(jnp.bfloat16), value_rows, preferred_element_type=jnp.float32)
            return (numerator / denominator[:, None]).astype(jnp.bfloat16)
        attended_heads = lax.map(one_head, jnp.arange(BLOCKS * QH, dtype=jnp.int32))
        attended_heads = attended_heads.reshape(BLOCKS, QH, BLOCK, HD).transpose(0, 2, 1, 3).reshape(SEQ, QH * HD)
        results.append(attended_heads)
    return jnp.stack(results)
```

```python
import math

import jax
import jax.numpy as jnp
from jax import lax
from jax.experimental import pallas as pl
from jax.experimental.pallas import tpu as pltpu
from jax.sharding import PartitionSpec as P

KVH = 8
HD = 128
QH = 16
STEPS = 3


LOG_BASE = math.log(500000.0)


def from_behind(block, axis, distance):
    devices = range(lax.axis_size(axis))
    route = [((i - distance) % len(devices), i) for i in devices]
    return lax.ppermute(block, axis, route)


def rotate(vectors, angle_table):
    half_dim = vectors.shape[-1] // 2
    first_half = vectors[..., :half_dim]
    second_half = vectors[..., half_dim:]
    cosine = jnp.cos(angle_table)
    sine_part = jnp.sin(angle_table)
    return jnp.concatenate(
        [
            first_half * cosine - second_half * sine_part,
            second_half * cosine + first_half * sine_part,
        ],
        axis=-1,
    )


def angles(positions, yarn_divisor):
    half_dim = yarn_divisor.shape[0]
    scaled = 2.0 * jnp.arange(half_dim, dtype=jnp.float32) / (2 * half_dim)
    inverse = jnp.exp(-LOG_BASE * scaled) / yarn_divisor.astype(jnp.float32)
    return positions.astype(jnp.float32)[:, None] * inverse[None, :]


def positions_of(order_row, first_row, row_count, span_rows):
    stored = first_row + jnp.arange(row_count, dtype=jnp.int32)
    span_index = stored // span_rows
    matches = span_index[:, None] == jnp.arange(order_row.shape[0], dtype=jnp.int32)[None, :]
    span_value = jnp.sum(jnp.where(matches, order_row[None, :], 0), axis=1)
    return span_value * span_rows + stored % span_rows


def tile_scores(query_rows, key_rows):
    product = lax.dot_general(
        query_rows, key_rows, (((1,), (1,)), ((), ())), preferred_element_type=jnp.float32
    )
    return product * (1.0 / math.sqrt(HD))


def row_maximum(query_rows, query_pos, key_rows, key_pos):
    score = tile_scores(query_rows, key_rows)
    return jnp.max(jnp.where(key_pos[None, :] <= query_pos[:, None], score, -jnp.inf), axis=1)


def add_tile(denominator, numerator, query_rows, query_pos, key_rows, value_rows, key_pos, row_top):
    score = tile_scores(query_rows, key_rows)
    allowed = key_pos[None, :] <= query_pos[:, None]
    weights = jnp.where(allowed, jnp.exp(score - row_top[:, None]), 0.0)
    denominator = denominator + jnp.sum(weights, axis=1)
    numerator = numerator + jnp.dot(
        weights.astype(jnp.bfloat16), value_rows, preferred_element_type=jnp.float32
    )
    return (denominator, numerator)


def general_shards(hidden_in, queries, pair_weight, span_order, yarn_divisor):
    inputs_local = hidden_in[0]
    queries_local = queries[0]
    order_row = span_order[0]
    token_rows = inputs_local.shape[0]
    ulysses_size = lax.axis_size("ulysses")
    cycle_size = lax.axis_size("blk")
    ulysses_index = lax.axis_index("ulysses")
    cycle_index = lax.axis_index("blk")
    block_rows = token_rows * ulysses_size
    span_rows = block_rows // 2
    kv_width = KVH * HD
    kv_local = KVH // ulysses_size
    group_size = QH // KVH
    own_positions = positions_of(
        order_row, cycle_index * block_rows + ulysses_index * token_rows, token_rows, span_rows
    )
    own_angles = angles(own_positions, yarn_divisor)
    block_positions = positions_of(order_row, cycle_index * block_rows, block_rows, span_rows)
    rotated_queries = rotate(
        queries_local.astype(jnp.float32).reshape(token_rows, QH, HD), own_angles[:, None, :]
    )
    rotated_queries = rotated_queries.astype(jnp.bfloat16).reshape(token_rows, QH * HD)
    projected = jnp.dot(
        inputs_local,
        lax.all_gather(pair_weight, ("dp", "blk"), axis=0, tiled=True),
        preferred_element_type=jnp.float32,
    )
    token_keys = rotate(
        projected[:, :kv_width].reshape(token_rows, KVH, HD), own_angles[:, None, :]
    )
    token_keys = token_keys.astype(jnp.bfloat16).reshape(token_rows, kv_width)
    token_values = projected[:, kv_width:].astype(jnp.bfloat16)
    query_block, key_block, value_block = (
        lax.all_to_all(rotated_queries, "ulysses", split_axis=1, concat_axis=0, tiled=True),
        lax.all_to_all(token_keys, "ulysses", split_axis=1, concat_axis=0, tiled=True),
        lax.all_to_all(token_values, "ulysses", split_axis=1, concat_axis=0, tiled=True),
    )
    own_pair = jnp.stack([key_block, value_block])
    carried_blocks = [own_pair]
    current_pair = own_pair
    for step_index in range(STEPS):
        current_pair = from_behind(current_pair, "blk", 1)
        carried_blocks.append(current_pair)
    carried_positions = []
    for step_index in range(STEPS + 1):
        source_block = jnp.remainder(cycle_index - step_index, cycle_size)
        carried_positions.append(
            positions_of(order_row, source_block * block_rows, block_rows, span_rows)
        )
    output_rows = []
    for query_half in range(2):
        row_start = query_half * span_rows
        half_positions = block_positions[row_start : row_start + span_rows]
        query_pos = jnp.tile(half_positions, group_size)
        head_outputs = []
        for local_head in range(kv_local):
            query_part = query_block[
                row_start : row_start + span_rows,
                local_head * group_size * HD : (local_head + 1) * group_size * HD,
            ]
            query_rows = (
                query_part.reshape(span_rows, group_size, HD)
                .transpose(1, 0, 2)
                .reshape(group_size * span_rows, HD)
            )
            tile_list = []
            for step_index in range(STEPS + 1):
                pair_block = carried_blocks[step_index]
                for key_half in range(2):
                    key_start = key_half * span_rows
                    key_rows = pair_block[
                        0,
                        key_start : key_start + span_rows,
                        local_head * HD : (local_head + 1) * HD,
                    ]
                    value_rows = pair_block[
                        1,
                        key_start : key_start + span_rows,
                        local_head * HD : (local_head + 1) * HD,
                    ]
                    key_pos = carried_positions[step_index][key_start : key_start + span_rows]
                    tile_list.append((key_rows, value_rows, key_pos))
            row_top = jnp.full((group_size * span_rows,), -jnp.inf, jnp.float32)
            for key_rows, value_rows, key_pos in tile_list:
                tile_top = row_maximum(query_rows, query_pos, key_rows, key_pos)
                row_top = jnp.maximum(row_top, tile_top)
            denominator = jnp.zeros((group_size * span_rows,), jnp.float32)
            numerator = jnp.zeros((group_size * span_rows, HD), jnp.float32)
            for key_rows, value_rows, key_pos in tile_list:
                denominator, numerator = add_tile(
                    denominator,
                    numerator,
                    query_rows,
                    query_pos,
                    key_rows,
                    value_rows,
                    key_pos,
                    row_top,
                )
            normalized = (numerator / denominator[:, None]).astype(jnp.bfloat16)
            normalized = (
                normalized.reshape(group_size, span_rows, HD)
                .transpose(1, 0, 2)
                .reshape(span_rows, group_size * HD)
            )
            head_outputs.append(normalized)
        output_rows.append(jnp.concatenate(head_outputs, axis=1))
    block_output = jnp.concatenate(output_rows, axis=0)
    token_output = lax.all_to_all(block_output, "ulysses", split_axis=0, concat_axis=1, tiled=True)
    return token_output[None]


def ring_route(dp_size, cycle_size):
    order = []
    for row in range(dp_size):
        steps = range(cycle_size) if row % 2 == 0 else reversed(range(cycle_size))
        order += [row * cycle_size + step for step in steps]
    return order


def swap(block, distance):
    size = lax.axis_size("ulysses")
    return lax.ppermute(block, "ulysses", [(i, i ^ distance) for i in range(size)])


def wide_tables(positions, yarn_divisor):
    angle_table = angles(positions, yarn_divisor)
    cosine, sine = jnp.cos(angle_table), jnp.sin(angle_table)
    return jnp.concatenate([cosine, cosine], axis=1), jnp.concatenate([-sine, sine], axis=1)


def rope_head(head, cosine, signed_sine):
    return head * cosine + pltpu.roll(head, HD // 2, 1) * signed_sine


def query_rope_kernel(head_order, query_ref, cosine_ref, sine_ref, out_ref):
    cosine, sine = cosine_ref[...], sine_ref[...]
    for place, head in enumerate(head_order):
        rows = query_ref[:, head * HD : (head + 1) * HD].astype(jnp.float32)
        out_ref[place] = rope_head(rows, cosine, sine).astype(jnp.bfloat16)


def pair_rope_kernel(total_ref, cosine_ref, sine_ref, out_ref):
    cosine, sine = cosine_ref[...], sine_ref[...]
    for head in range(out_ref.shape[0]):
        rows = total_ref[:, head * HD : (head + 1) * HD]
        out_ref[head] = rope_head(rows, cosine, sine).astype(jnp.bfloat16)


def order_heads_kernel(head_order, block_ref, out_ref):
    for place, head in enumerate(head_order):
        out_ref[:, head * HD : (head + 1) * HD] = block_ref[place]


def attention_kernel(order_ref, place_ref, query_ref, mine_ref, theirs_ref, out_ref, key_rows, value_rows):
    spans = order_ref.shape[1]
    sources, token_rows = query_ref.shape[0], query_ref.shape[2]
    per_span = sources // 2
    span_rows = per_span * token_rows
    place = place_ref[0]
    keys_here = place % 2 == 0
    stored = []
    for position in range(spans):
        span = jnp.int32(0)
        for candidate in range(1, spans):
            span = jnp.where(order_ref[0, candidate] == position, candidate, span)
        stored.append((span // 2, span % 2))
    for position, (block, half) in enumerate(stored):
        for part in range(per_span):
            slot = jnp.bitwise_xor(half * per_span + part, place)
            other = jnp.bitwise_xor(slot, 1)
            mine = mine_ref[block, pl.ds(pl.multiple_of(slot * token_rows, token_rows), token_rows), :]
            theirs = theirs_ref[block, pl.ds(pl.multiple_of(other * token_rows, token_rows), token_rows), :]
            rows = pl.ds(position * span_rows + part * token_rows, token_rows)
            key_rows[rows, :] = jnp.where(keys_here, mine, theirs)
            value_rows[rows, :] = jnp.where(keys_here, theirs, mine)
    row_index = lax.broadcasted_iota(jnp.int32, (span_rows, span_rows), 0)
    column_index = lax.broadcasted_iota(jnp.int32, (span_rows, span_rows), 1)
    for position, (block, half) in enumerate(stored):
        query = query_ref[pl.ds(half * per_span, per_span), block].reshape(span_rows, HD)
        reach = (position + 1) * span_rows
        score = tile_scores(query, key_rows[:reach, :])
        last = jnp.where(column_index <= row_index, score[:, position * span_rows :], -jnp.inf)
        score = jnp.concatenate([score[:, : position * span_rows], last], axis=1) if position else last
        row_top = jnp.max(score, axis=1, keepdims=True)
        weights = jnp.exp(score - row_top)
        denominator = jnp.sum(weights, axis=1, keepdims=True)
        numerator = jnp.dot(
            weights.astype(jnp.bfloat16), value_rows[:reach, :], preferred_element_type=jnp.float32
        )
        rows = (numerator / denominator).astype(jnp.bfloat16)
        out_ref[pl.ds(half * per_span, per_span), block] = rows.reshape(per_span, token_rows, HD)


VMEM = pl.BlockSpec(memory_space=pltpu.VMEM)
SMEM = pl.BlockSpec(memory_space=pltpu.SMEM)


def whole_cycle_shards(hidden_in, queries, pair_weight, span_order, yarn_divisor):
    own_hidden = hidden_in[0]
    token_rows = own_hidden.shape[0]
    ulysses_size, cycle_size = lax.axis_size("ulysses"), lax.axis_size("blk")
    dp_size = lax.axis_size("dp")
    ulysses_index, cycle_index = lax.axis_index("ulysses"), lax.axis_index("blk")
    dp_index = lax.axis_index("dp")
    block_rows = token_rows * ulysses_size
    span_rows = block_rows // 2
    shard_rows = pair_weight.shape[0]
    kv_width = KVH * HD
    columns = cycle_size * HD
    core, chip = ulysses_index % 2, ulysses_index // 2

    piece = lax.dynamic_slice(
        pair_weight, (0, core * kv_width + chip * columns), (shard_rows, columns)
    )
    order = ring_route(dp_size, cycle_size)
    shards_total = len(order)
    forward = [(order[i], order[(i + 1) % shards_total]) for i in range(shards_total)]
    backward = [(target, source) for source, target in forward]
    walked = jnp.where(dp_index % 2 == 0, cycle_index, cycle_size - 1 - cycle_index)
    ring_place = dp_index * cycle_size + walked

    def shard_at(place):
        place = jnp.remainder(place, shards_total)
        row, step = place // cycle_size, place % cycle_size
        return row * cycle_size + jnp.where(row % 2 == 0, step, cycle_size - 1 - step)

    partner = swap(own_hidden, 1)
    slots = [own_hidden, partner]
    for distance in range(2, ulysses_size, 2):
        far = swap(own_hidden, distance)
        slots += [far, swap(far, 1)]
    hidden = jnp.concatenate(slots, axis=0)

    def term(weight_rows, first_row):
        left = lax.dynamic_slice(hidden, (0, first_row), (block_rows, weight_rows.shape[0]))
        return jnp.dot(left, weight_rows, preferred_element_type=jnp.float32)

    total = term(piece, shard_at(ring_place) * shard_rows)
    ahead = behind = piece
    for step in range(1, shards_total // 2):
        ahead = lax.ppermute(ahead, ("dp", "blk"), forward)
        behind = lax.ppermute(behind, ("dp", "blk"), backward)
        total = total + term(ahead, shard_at(ring_place - step) * shard_rows)
        total = total + term(behind, shard_at(ring_place + step) * shard_rows)
    half_rows = shard_rows // 2
    opposite = shard_at(ring_place + shards_total // 2) * shard_rows
    ahead = lax.ppermute(ahead[:half_rows], ("dp", "blk"), forward)
    behind = lax.ppermute(behind[half_rows:], ("dp", "blk"), backward)
    total = total + term(ahead, opposite)
    total = total + term(behind, opposite + half_rows)

    slot_devices = jnp.bitwise_xor(ulysses_index, jnp.arange(ulysses_size, dtype=jnp.int32))
    order_row = span_order[0]
    span_values = lax.dynamic_slice(order_row, (2 * cycle_index,), (2,))
    stored = slot_devices[:, None] * token_rows + jnp.arange(token_rows, dtype=jnp.int32)[None, :]
    stored = stored.reshape(block_rows)
    positions = jnp.where(stored < span_rows, span_values[0], span_values[1]) * span_rows + stored % span_rows
    cosine, sine = wide_tables(positions, yarn_divisor)
    own_cosine, own_sine = cosine[:token_rows], sine[:token_rows]
    pair_cosine = jnp.where(core == 0, cosine, 1.0)
    pair_sine = jnp.where(core == 0, sine, 0.0)

    head_order = [
        (chip_place * cycle_size + block) * 2 + core_place
        for chip_place in range(ulysses_size // 2)
        for core_place in range(2)
        for block in range(cycle_size)
    ]
    rotated = pl.pallas_call(
        lambda *refs: query_rope_kernel(head_order, *refs),
        out_shape=jax.ShapeDtypeStruct((QH, token_rows, HD), jnp.bfloat16),
        in_specs=[VMEM] * 3,
        out_specs=VMEM,
        name="query_rope",
    )(queries[0], own_cosine, own_sine)
    query_rows = lax.all_to_all(rotated, ("ulysses", "blk"), split_axis=0, concat_axis=0, tiled=True)
    query_rows = query_rows.reshape(ulysses_size, cycle_size, token_rows, HD)

    pair = pl.pallas_call(
        pair_rope_kernel,
        out_shape=jax.ShapeDtypeStruct((cycle_size, block_rows, HD), jnp.bfloat16),
        in_specs=[VMEM] * 3,
        out_specs=VMEM,
        name="pair_rope",
    )(total, pair_cosine, pair_sine)
    mine = lax.all_to_all(pair, "blk", split_axis=0, concat_axis=0, tiled=True)
    theirs = swap(mine, 1)

    sequence_rows = cycle_size * block_rows
    attended = pl.pallas_call(
        attention_kernel,
        out_shape=jax.ShapeDtypeStruct((ulysses_size, cycle_size, token_rows, HD), jnp.bfloat16),
        in_specs=[SMEM, SMEM, VMEM, VMEM, VMEM],
        out_specs=VMEM,
        scratch_shapes=[
            pltpu.VMEM((sequence_rows, HD), jnp.bfloat16),
            pltpu.VMEM((sequence_rows, HD), jnp.bfloat16),
        ],
        compiler_params=pltpu.CompilerParams(vmem_limit_bytes=40 * 1024 * 1024),
        name="attention",
    )(span_order, ulysses_index.astype(jnp.int32).reshape(1), query_rows, mine, theirs)
    heads = lax.all_to_all(
        attended.reshape(QH, token_rows, HD), ("ulysses", "blk"), split_axis=0, concat_axis=0, tiled=True
    )
    rows = pl.pallas_call(
        lambda *refs: order_heads_kernel(head_order, *refs),
        out_shape=jax.ShapeDtypeStruct((token_rows, QH * HD), jnp.bfloat16),
        in_specs=[VMEM],
        out_specs=VMEM,
        name="order_heads",
    )(heads)
    return rows[None]


def solution(mesh):
    sizes = dict(mesh.shape)
    whole_cycle = (
        sizes["blk"] == STEPS + 1
        and sizes["ulysses"] * sizes["blk"] == QH
        and QH == 2 * KVH
        and sizes["ulysses"] & (sizes["ulysses"] - 1) == 0
        and sizes["dp"] % 2 == 0
    )
    return jax.shard_map(
        whole_cycle_shards if whole_cycle else general_shards,
        mesh=mesh,
        in_specs=(
            P("dp", ("blk", "ulysses"), None),
            P("dp", ("blk", "ulysses"), None),
            P(("dp", "blk"), None),
            P("dp", None),
            P(),
        ),
        out_specs=P("dp", ("blk", "ulysses"), None),
        check_vma=False,
    )
```

```python
import math

import jax
import jax.numpy as jnp
from jax import lax
from jax.experimental import pallas as pl
from jax.experimental.pallas import tpu as pltpu
from jax.sharding import PartitionSpec as P

KVH = 8
HD = 128
QH = 16
STEPS = 3


LOG_BASE = math.log(500000.0)


def from_behind(block, axis, distance):
    devices = range(lax.axis_size(axis))
    route = [((i - distance) % len(devices), i) for i in devices]
    return lax.ppermute(block, axis, route)


def rotate(vectors, angle_table):
    half_dim = vectors.shape[-1] // 2
    first_half = vectors[..., :half_dim]
    second_half = vectors[..., half_dim:]
    cosine = jnp.cos(angle_table)
    sine_part = jnp.sin(angle_table)
    return jnp.concatenate(
        [
            first_half * cosine - second_half * sine_part,
            second_half * cosine + first_half * sine_part,
        ],
        axis=-1,
    )


def angles(positions, yarn_divisor):
    half_dim = yarn_divisor.shape[0]
    scaled = 2.0 * jnp.arange(half_dim, dtype=jnp.float32) / (2 * half_dim)
    inverse = jnp.exp(-LOG_BASE * scaled) / yarn_divisor.astype(jnp.float32)
    return positions.astype(jnp.float32)[:, None] * inverse[None, :]


def positions_of(order_row, first_row, row_count, span_rows):
    stored = first_row + jnp.arange(row_count, dtype=jnp.int32)
    span_index = stored // span_rows
    matches = span_index[:, None] == jnp.arange(order_row.shape[0], dtype=jnp.int32)[None, :]
    span_value = jnp.sum(jnp.where(matches, order_row[None, :], 0), axis=1)
    return span_value * span_rows + stored % span_rows


def tile_scores(query_rows, key_rows):
    product = lax.dot_general(
        query_rows, key_rows, (((1,), (1,)), ((), ())), preferred_element_type=jnp.float32
    )
    return product * (1.0 / math.sqrt(HD))


def row_maximum(query_rows, query_pos, key_rows, key_pos):
    score = tile_scores(query_rows, key_rows)
    return jnp.max(jnp.where(key_pos[None, :] <= query_pos[:, None], score, -jnp.inf), axis=1)


def add_tile(denominator, numerator, query_rows, query_pos, key_rows, value_rows, key_pos, row_top):
    score = tile_scores(query_rows, key_rows)
    allowed = key_pos[None, :] <= query_pos[:, None]
    weights = jnp.where(allowed, jnp.exp(score - row_top[:, None]), 0.0)
    denominator = denominator + jnp.sum(weights, axis=1)
    numerator = numerator + jnp.dot(
        weights.astype(jnp.bfloat16), value_rows, preferred_element_type=jnp.float32
    )
    return (denominator, numerator)


def general_shards(hidden_in, queries, pair_weight, span_order, yarn_divisor):
    inputs_local = hidden_in[0]
    queries_local = queries[0]
    order_row = span_order[0]
    token_rows = inputs_local.shape[0]
    ulysses_size = lax.axis_size("ulysses")
    cycle_size = lax.axis_size("blk")
    ulysses_index = lax.axis_index("ulysses")
    cycle_index = lax.axis_index("blk")
    block_rows = token_rows * ulysses_size
    span_rows = block_rows // 2
    kv_width = KVH * HD
    kv_local = KVH // ulysses_size
    group_size = QH // KVH
    own_positions = positions_of(
        order_row, cycle_index * block_rows + ulysses_index * token_rows, token_rows, span_rows
    )
    own_angles = angles(own_positions, yarn_divisor)
    block_positions = positions_of(order_row, cycle_index * block_rows, block_rows, span_rows)
    rotated_queries = rotate(
        queries_local.astype(jnp.float32).reshape(token_rows, QH, HD), own_angles[:, None, :]
    )
    rotated_queries = rotated_queries.astype(jnp.bfloat16).reshape(token_rows, QH * HD)
    projected = jnp.dot(
        inputs_local,
        lax.all_gather(pair_weight, ("dp", "blk"), axis=0, tiled=True),
        preferred_element_type=jnp.float32,
    )
    token_keys = rotate(
        projected[:, :kv_width].reshape(token_rows, KVH, HD), own_angles[:, None, :]
    )
    token_keys = token_keys.astype(jnp.bfloat16).reshape(token_rows, kv_width)
    token_values = projected[:, kv_width:].astype(jnp.bfloat16)
    query_block, key_block, value_block = (
        lax.all_to_all(rotated_queries, "ulysses", split_axis=1, concat_axis=0, tiled=True),
        lax.all_to_all(token_keys, "ulysses", split_axis=1, concat_axis=0, tiled=True),
        lax.all_to_all(token_values, "ulysses", split_axis=1, concat_axis=0, tiled=True),
    )
    own_pair = jnp.stack([key_block, value_block])
    carried_blocks = [own_pair]
    current_pair = own_pair
    for step_index in range(STEPS):
        current_pair = from_behind(current_pair, "blk", 1)
        carried_blocks.append(current_pair)
    carried_positions = []
    for step_index in range(STEPS + 1):
        source_block = jnp.remainder(cycle_index - step_index, cycle_size)
        carried_positions.append(
            positions_of(order_row, source_block * block_rows, block_rows, span_rows)
        )
    output_rows = []
    for query_half in range(2):
        row_start = query_half * span_rows
        half_positions = block_positions[row_start : row_start + span_rows]
        query_pos = jnp.tile(half_positions, group_size)
        head_outputs = []
        for local_head in range(kv_local):
            query_part = query_block[
                row_start : row_start + span_rows,
                local_head * group_size * HD : (local_head + 1) * group_size * HD,
            ]
            query_rows = (
                query_part.reshape(span_rows, group_size, HD)
                .transpose(1, 0, 2)
                .reshape(group_size * span_rows, HD)
            )
            tile_list = []
            for step_index in range(STEPS + 1):
                pair_block = carried_blocks[step_index]
                for key_half in range(2):
                    key_start = key_half * span_rows
                    key_rows = pair_block[
                        0,
                        key_start : key_start + span_rows,
                        local_head * HD : (local_head + 1) * HD,
                    ]
                    value_rows = pair_block[
                        1,
                        key_start : key_start + span_rows,
                        local_head * HD : (local_head + 1) * HD,
                    ]
                    key_pos = carried_positions[step_index][key_start : key_start + span_rows]
                    tile_list.append((key_rows, value_rows, key_pos))
            row_top = jnp.full((group_size * span_rows,), -jnp.inf, jnp.float32)
            for key_rows, value_rows, key_pos in tile_list:
                tile_top = row_maximum(query_rows, query_pos, key_rows, key_pos)
                row_top = jnp.maximum(row_top, tile_top)
            denominator = jnp.zeros((group_size * span_rows,), jnp.float32)
            numerator = jnp.zeros((group_size * span_rows, HD), jnp.float32)
            for key_rows, value_rows, key_pos in tile_list:
                denominator, numerator = add_tile(
                    denominator,
                    numerator,
                    query_rows,
                    query_pos,
                    key_rows,
                    value_rows,
                    key_pos,
                    row_top,
                )
            normalized = (numerator / denominator[:, None]).astype(jnp.bfloat16)
            normalized = (
                normalized.reshape(group_size, span_rows, HD)
                .transpose(1, 0, 2)
                .reshape(span_rows, group_size * HD)
            )
            head_outputs.append(normalized)
        output_rows.append(jnp.concatenate(head_outputs, axis=1))
    block_output = jnp.concatenate(output_rows, axis=0)
    token_output = lax.all_to_all(block_output, "ulysses", split_axis=0, concat_axis=1, tiled=True)
    return token_output[None]


def swap(block, distance):
    size = lax.axis_size("ulysses")
    return lax.ppermute(block, "ulysses", [(i, i ^ distance) for i in range(size)])


def wide_tables(positions, yarn_divisor):
    angle_table = angles(positions, yarn_divisor)
    cosine, sine = jnp.cos(angle_table), jnp.sin(angle_table)
    return jnp.concatenate([cosine, cosine], axis=1), jnp.concatenate([-sine, sine], axis=1)


def rope_head(head, cosine, signed_sine):
    return head * cosine + pltpu.roll(head, HD // 2, 1) * signed_sine


def query_rope_kernel(head_order, query_ref, cosine_ref, sine_ref, out_ref):
    cosine, sine = cosine_ref[...], sine_ref[...]
    for place, head in enumerate(head_order):
        rows = query_ref[:, head * HD : (head + 1) * HD].astype(jnp.float32)
        out_ref[place] = rope_head(rows, cosine, sine).astype(jnp.bfloat16)


def pair_rope_kernel(block_ref, total_ref, hidden_ref, weight_ref, cosine_ref, sine_ref, *refs):
    out_refs, sum_ref = refs[:-1], refs[-1]
    sum_ref[...] = total_ref[...] + jnp.dot(
        hidden_ref[...], weight_ref[...], preferred_element_type=jnp.float32
    )
    cosine, sine = cosine_ref[...], sine_ref[...]
    for distance, out_ref in enumerate(out_refs):
        head = lax.rem(block_ref[0] + distance, len(out_refs))
        rows = sum_ref[:, pl.ds(pl.multiple_of(head * HD, HD), HD)]
        out_ref[...] = rope_head(rows, cosine, sine).astype(jnp.bfloat16)


def order_heads_kernel(head_order, block_ref, out_ref):
    for place, head in enumerate(head_order):
        out_ref[:, head * HD : (head + 1) * HD] = block_ref[place]


def attention_kernel(order_ref, place_ref, query_ref, *refs):
    spans = order_ref.shape[1]
    blocks = spans // 2
    mine_refs, theirs_refs = refs[:blocks], refs[blocks : 2 * blocks]
    out_ref, key_rows, value_rows = refs[2 * blocks :]
    sources, token_rows = query_ref.shape[0], query_ref.shape[2]
    per_span = sources // 2
    span_rows = per_span * token_rows
    place, block_here = place_ref[0], place_ref[1]
    keys_here = place % 2 == 0
    for distance in range(blocks):
        block = lax.rem(block_here + blocks - distance, blocks)
        for half in range(2):
            first = order_ref[0, 2 * block + half] * span_rows
            for part in range(per_span):
                slot = jnp.bitwise_xor(half * per_span + part, place)
                other = jnp.bitwise_xor(slot, 1)
                mine = mine_refs[distance][pl.ds(pl.multiple_of(slot * token_rows, token_rows), token_rows), :]
                theirs = theirs_refs[distance][
                    pl.ds(pl.multiple_of(other * token_rows, token_rows), token_rows), :
                ]
                rows = pl.ds(pl.multiple_of(first + part * token_rows, token_rows), token_rows)
                key_rows[rows, :] = jnp.where(keys_here, mine, theirs)
                value_rows[rows, :] = jnp.where(keys_here, theirs, mine)
    stored = []
    for position in range(spans):
        span = jnp.int32(0)
        for candidate in range(1, spans):
            span = jnp.where(order_ref[0, candidate] == position, candidate, span)
        stored.append((span // 2, span % 2))
    row_index = lax.broadcasted_iota(jnp.int32, (span_rows, span_rows), 0)
    column_index = lax.broadcasted_iota(jnp.int32, (span_rows, span_rows), 1)
    for position, (block, half) in enumerate(stored):
        query = query_ref[pl.ds(half * per_span, per_span), block].reshape(span_rows, HD)
        reach = (position + 1) * span_rows
        score = tile_scores(query, key_rows[:reach, :])
        last = jnp.where(column_index <= row_index, score[:, position * span_rows :], -jnp.inf)
        score = jnp.concatenate([score[:, : position * span_rows], last], axis=1) if position else last
        row_top = jnp.max(score, axis=1, keepdims=True)
        weights = jnp.exp(score - row_top)
        denominator = jnp.sum(weights, axis=1, keepdims=True)
        numerator = jnp.dot(
            weights.astype(jnp.bfloat16), value_rows[:reach, :], preferred_element_type=jnp.float32
        )
        rows = (numerator / denominator).astype(jnp.bfloat16)
        out_ref[pl.ds(half * per_span, per_span), block] = rows.reshape(per_span, token_rows, HD)


VMEM = pl.BlockSpec(memory_space=pltpu.VMEM)
SMEM = pl.BlockSpec(memory_space=pltpu.SMEM)


def whole_cycle_shards(hidden_in, queries, pair_weight, span_order, yarn_divisor):
    own_hidden = hidden_in[0]
    token_rows = own_hidden.shape[0]
    ulysses_size, cycle_size = lax.axis_size("ulysses"), lax.axis_size("blk")
    dp_size = lax.axis_size("dp")
    ulysses_index, cycle_index = lax.axis_index("ulysses"), lax.axis_index("blk")
    dp_index = lax.axis_index("dp")
    block_rows = token_rows * ulysses_size
    span_rows = block_rows // 2
    shard_rows = pair_weight.shape[0]
    kv_width = KVH * HD
    columns = cycle_size * HD
    core, chip = ulysses_index % 2, ulysses_index // 2

    piece = lax.dynamic_slice(
        pair_weight, (0, core * kv_width + chip * columns), (shard_rows, columns)
    )
    slot_devices = jnp.bitwise_xor(ulysses_index, jnp.arange(ulysses_size, dtype=jnp.int32))
    order_row = span_order[0]
    span_values = lax.dynamic_slice(order_row, (2 * cycle_index,), (2,))
    stored = slot_devices[:, None] * token_rows + jnp.arange(token_rows, dtype=jnp.int32)[None, :]
    stored = stored.reshape(block_rows)
    positions = jnp.where(stored < span_rows, span_values[0], span_values[1]) * span_rows + stored % span_rows
    cosine, sine = wide_tables(positions, yarn_divisor)
    own_cosine, own_sine = cosine[:token_rows], sine[:token_rows]
    pair_cosine = jnp.where(core == 0, cosine, 1.0)
    pair_sine = jnp.where(core == 0, sine, 0.0)

    head_order = [
        (chip_place * cycle_size + block) * 2 + core_place
        for chip_place in range(ulysses_size // 2)
        for core_place in range(2)
        for block in range(cycle_size)
    ]
    rotated = pl.pallas_call(
        lambda *refs: query_rope_kernel(head_order, *refs),
        out_shape=jax.ShapeDtypeStruct((QH, token_rows, HD), jnp.bfloat16),
        in_specs=[VMEM] * 3,
        out_specs=VMEM,
        compiler_params=pltpu.CompilerParams(vmem_limit_bytes=8 * 1024 * 1024),
        name="query_rope",
    )(queries[0], own_cosine, own_sine)
    def ahead(block, distance=1):
        return lax.ppermute(block, "blk", [(i, (i + distance) % cycle_size) for i in range(cycle_size)])

    def across(block):
        return lax.ppermute(block, "dp", [(i, dp_size - 1 - i) for i in range(dp_size)])

    def first_row(distance, row):
        return (row * cycle_size + jnp.remainder(cycle_index - distance, cycle_size)) * shard_rows

    other_row = dp_size - 1 - dp_index
    far_slots = [swap(own_hidden, distance) for distance in range(2, ulysses_size, 2)]
    partner = swap(own_hidden, 1)
    crossed = across(piece)
    received = [(piece, first_row(0, dp_index))]
    travelling = piece
    hidden = total = None

    def add_terms(total, received):
        for rows, row in received:
            left = lax.dynamic_slice(hidden, (0, row), (block_rows, shard_rows))
            term = jnp.dot(left, rows, preferred_element_type=jnp.float32)
            total = term if total is None else total + term
        return total

    for distance in range(1, cycle_size):
        travelling = ahead(travelling)
        if distance == cycle_size - 1:
            total = add_terms(total, received)
            received = []
            travelling, total = lax.optimization_barrier((travelling, total))
        if distance == 1:
            rotated, pair_cosine, pair_sine, travelling = lax.optimization_barrier(
                (rotated, pair_cosine, pair_sine, travelling)
            )
        travelling, crossed = lax.optimization_barrier((travelling, crossed))
        received += [
            (crossed, first_row(distance - 1, other_row)),
            (travelling, first_row(distance, dp_index)),
        ]
        crossed = across(travelling)
        if distance == cycle_size - 2:
            *far_slots, travelling = lax.optimization_barrier((*far_slots, travelling))
            slots = [own_hidden, partner]
            for far in far_slots:
                slots += [far, swap(far, 1)]
            hidden = jnp.concatenate(slots, axis=0)
    received.append((crossed, first_row(cycle_size - 1, other_row)))
    last_piece, last_row = received.pop()
    total = add_terms(total, received)
    rotated, travelling = lax.optimization_barrier((rotated, travelling))
    query_rows = lax.all_to_all(rotated, ("ulysses", "blk"), split_axis=0, concat_axis=0, tiled=True)
    query_rows = query_rows.reshape(ulysses_size, cycle_size, token_rows, HD)
    last_hidden = lax.dynamic_slice(hidden, (0, last_row), (block_rows, shard_rows))
    last_piece, total, last_hidden = lax.optimization_barrier((last_piece, total, last_hidden))

    *pairs, = pl.pallas_call(
        pair_rope_kernel,
        out_shape=[jax.ShapeDtypeStruct((block_rows, HD), jnp.bfloat16)] * cycle_size,
        in_specs=[SMEM] + [VMEM] * 5,
        out_specs=[VMEM] * cycle_size,
        scratch_shapes=[pltpu.VMEM((block_rows, columns), jnp.float32)],
        compiler_params=pltpu.CompilerParams(vmem_limit_bytes=12 * 1024 * 1024),
        name="pair_rope",
    )(cycle_index.astype(jnp.int32).reshape(1), total, last_hidden, last_piece, pair_cosine, pair_sine)
    *pairs, query_rows = lax.optimization_barrier((*pairs, query_rows))
    mine, theirs = [pairs[0]] + [None] * (cycle_size - 1), [swap(pairs[0], 1)] + [None] * (cycle_size - 1)
    for distance in sorted(range(1, cycle_size), key=lambda d: -min(d, cycle_size - d)):
        mine[distance] = ahead(pairs[distance], distance)
        theirs[distance] = swap(mine[distance], 1)

    sequence_rows = cycle_size * block_rows
    attended = pl.pallas_call(
        attention_kernel,
        out_shape=jax.ShapeDtypeStruct((ulysses_size, cycle_size, token_rows, HD), jnp.bfloat16),
        in_specs=[SMEM, SMEM] + [VMEM] * (1 + 2 * cycle_size),
        out_specs=VMEM,
        scratch_shapes=[
            pltpu.VMEM((sequence_rows, HD), jnp.bfloat16),
            pltpu.VMEM((sequence_rows, HD), jnp.bfloat16),
        ],
        compiler_params=pltpu.CompilerParams(vmem_limit_bytes=24 * 1024 * 1024),
        name="attention",
    )(span_order, jnp.stack([ulysses_index, cycle_index]).astype(jnp.int32), query_rows, *mine, *theirs)
    heads = lax.all_to_all(
        attended.reshape(QH, token_rows, HD), ("ulysses", "blk"), split_axis=0, concat_axis=0, tiled=True
    )
    rows = pl.pallas_call(
        lambda *refs: order_heads_kernel(head_order, *refs),
        out_shape=jax.ShapeDtypeStruct((token_rows, QH * HD), jnp.bfloat16),
        in_specs=[VMEM],
        out_specs=VMEM,
        compiler_params=pltpu.CompilerParams(vmem_limit_bytes=8 * 1024 * 1024),
        name="order_heads",
    )(heads)
    return rows[None]


def solution(mesh):
    sizes = dict(mesh.shape)
    whole_cycle = (
        sizes["blk"] == STEPS + 1
        and sizes["ulysses"] * sizes["blk"] == QH
        and QH == 2 * KVH
        and sizes["ulysses"] & (sizes["ulysses"] - 1) == 0
        and sizes["dp"] == 2
    )
    return jax.shard_map(
        whole_cycle_shards if whole_cycle else general_shards,
        mesh=mesh,
        in_specs=(
            P("dp", ("blk", "ulysses"), None),
            P("dp", ("blk", "ulysses"), None),
            P(("dp", "blk"), None),
            P("dp", None),
            P(),
        ),
        out_specs=P("dp", ("blk", "ulysses"), None),
        check_vma=False,
    )
```

```python
import functools
import math

import jax
import jax.numpy as jnp
from jax import lax
from jax.experimental import pallas as pl
from jax.experimental.pallas import tpu as pltpu
from jax.sharding import PartitionSpec as P

KVH = 8
HD = 128
QH = 16
STEPS = 3


LOG_BASE = math.log(500000.0)


def from_behind(block, axis, distance):
    devices = range(lax.axis_size(axis))
    route = [((i - distance) % len(devices), i) for i in devices]
    return lax.ppermute(block, axis, route)


def rotate(vectors, angle_table):
    half_dim = vectors.shape[-1] // 2
    first_half = vectors[..., :half_dim]
    second_half = vectors[..., half_dim:]
    cosine = jnp.cos(angle_table)
    sine_part = jnp.sin(angle_table)
    return jnp.concatenate(
        [
            first_half * cosine - second_half * sine_part,
            second_half * cosine + first_half * sine_part,
        ],
        axis=-1,
    )


def angles(positions, yarn_divisor):
    half_dim = yarn_divisor.shape[0]
    scaled = 2.0 * jnp.arange(half_dim, dtype=jnp.float32) / (2 * half_dim)
    inverse = jnp.exp(-LOG_BASE * scaled) / yarn_divisor.astype(jnp.float32)
    return positions.astype(jnp.float32)[:, None] * inverse[None, :]


def positions_of(order_row, first_row, row_count, span_rows):
    stored = first_row + jnp.arange(row_count, dtype=jnp.int32)
    span_index = stored // span_rows
    matches = span_index[:, None] == jnp.arange(order_row.shape[0], dtype=jnp.int32)[None, :]
    span_value = jnp.sum(jnp.where(matches, order_row[None, :], 0), axis=1)
    return span_value * span_rows + stored % span_rows


def tile_scores(query_rows, key_rows):
    product = lax.dot_general(
        query_rows, key_rows, (((1,), (1,)), ((), ())), preferred_element_type=jnp.float32
    )
    return product * (1.0 / math.sqrt(HD))


def row_maximum(query_rows, query_pos, key_rows, key_pos):
    score = tile_scores(query_rows, key_rows)
    return jnp.max(jnp.where(key_pos[None, :] <= query_pos[:, None], score, -jnp.inf), axis=1)


def add_tile(denominator, numerator, query_rows, query_pos, key_rows, value_rows, key_pos, row_top):
    score = tile_scores(query_rows, key_rows)
    allowed = key_pos[None, :] <= query_pos[:, None]
    weights = jnp.where(allowed, jnp.exp(score - row_top[:, None]), 0.0)
    denominator = denominator + jnp.sum(weights, axis=1)
    numerator = numerator + jnp.dot(
        weights.astype(jnp.bfloat16), value_rows, preferred_element_type=jnp.float32
    )
    return (denominator, numerator)


def general_shards(hidden_in, queries, pair_weight, span_order, yarn_divisor):
    inputs_local = hidden_in[0]
    queries_local = queries[0]
    order_row = span_order[0]
    token_rows = inputs_local.shape[0]
    ulysses_size = lax.axis_size("ulysses")
    cycle_size = lax.axis_size("blk")
    ulysses_index = lax.axis_index("ulysses")
    cycle_index = lax.axis_index("blk")
    block_rows = token_rows * ulysses_size
    span_rows = block_rows // 2
    kv_width = KVH * HD
    kv_local = KVH // ulysses_size
    group_size = QH // KVH
    own_positions = positions_of(
        order_row, cycle_index * block_rows + ulysses_index * token_rows, token_rows, span_rows
    )
    own_angles = angles(own_positions, yarn_divisor)
    block_positions = positions_of(order_row, cycle_index * block_rows, block_rows, span_rows)
    rotated_queries = rotate(
        queries_local.astype(jnp.float32).reshape(token_rows, QH, HD), own_angles[:, None, :]
    )
    rotated_queries = rotated_queries.astype(jnp.bfloat16).reshape(token_rows, QH * HD)
    projected = jnp.dot(
        inputs_local,
        lax.all_gather(pair_weight, ("dp", "blk"), axis=0, tiled=True),
        preferred_element_type=jnp.float32,
    )
    token_keys = rotate(
        projected[:, :kv_width].reshape(token_rows, KVH, HD), own_angles[:, None, :]
    )
    token_keys = token_keys.astype(jnp.bfloat16).reshape(token_rows, kv_width)
    token_values = projected[:, kv_width:].astype(jnp.bfloat16)
    query_block, key_block, value_block = (
        lax.all_to_all(rotated_queries, "ulysses", split_axis=1, concat_axis=0, tiled=True),
        lax.all_to_all(token_keys, "ulysses", split_axis=1, concat_axis=0, tiled=True),
        lax.all_to_all(token_values, "ulysses", split_axis=1, concat_axis=0, tiled=True),
    )
    own_pair = jnp.stack([key_block, value_block])
    carried_blocks = [own_pair]
    current_pair = own_pair
    for step_index in range(STEPS):
        current_pair = from_behind(current_pair, "blk", 1)
        carried_blocks.append(current_pair)
    carried_positions = []
    for step_index in range(STEPS + 1):
        source_block = jnp.remainder(cycle_index - step_index, cycle_size)
        carried_positions.append(
            positions_of(order_row, source_block * block_rows, block_rows, span_rows)
        )
    output_rows = []
    for query_half in range(2):
        row_start = query_half * span_rows
        half_positions = block_positions[row_start : row_start + span_rows]
        query_pos = jnp.tile(half_positions, group_size)
        head_outputs = []
        for local_head in range(kv_local):
            query_part = query_block[
                row_start : row_start + span_rows,
                local_head * group_size * HD : (local_head + 1) * group_size * HD,
            ]
            query_rows = (
                query_part.reshape(span_rows, group_size, HD)
                .transpose(1, 0, 2)
                .reshape(group_size * span_rows, HD)
            )
            tile_list = []
            for step_index in range(STEPS + 1):
                pair_block = carried_blocks[step_index]
                for key_half in range(2):
                    key_start = key_half * span_rows
                    key_rows = pair_block[
                        0,
                        key_start : key_start + span_rows,
                        local_head * HD : (local_head + 1) * HD,
                    ]
                    value_rows = pair_block[
                        1,
                        key_start : key_start + span_rows,
                        local_head * HD : (local_head + 1) * HD,
                    ]
                    key_pos = carried_positions[step_index][key_start : key_start + span_rows]
                    tile_list.append((key_rows, value_rows, key_pos))
            row_top = jnp.full((group_size * span_rows,), -jnp.inf, jnp.float32)
            for key_rows, value_rows, key_pos in tile_list:
                tile_top = row_maximum(query_rows, query_pos, key_rows, key_pos)
                row_top = jnp.maximum(row_top, tile_top)
            denominator = jnp.zeros((group_size * span_rows,), jnp.float32)
            numerator = jnp.zeros((group_size * span_rows, HD), jnp.float32)
            for key_rows, value_rows, key_pos in tile_list:
                denominator, numerator = add_tile(
                    denominator,
                    numerator,
                    query_rows,
                    query_pos,
                    key_rows,
                    value_rows,
                    key_pos,
                    row_top,
                )
            normalized = (numerator / denominator[:, None]).astype(jnp.bfloat16)
            normalized = (
                normalized.reshape(group_size, span_rows, HD)
                .transpose(1, 0, 2)
                .reshape(span_rows, group_size * HD)
            )
            head_outputs.append(normalized)
        output_rows.append(jnp.concatenate(head_outputs, axis=1))
    block_output = jnp.concatenate(output_rows, axis=0)
    token_output = lax.all_to_all(block_output, "ulysses", split_axis=0, concat_axis=1, tiled=True)
    return token_output[None]


def swap(block, distance):
    size = lax.axis_size("ulysses")
    return lax.ppermute(block, "ulysses", [(i, i ^ distance) for i in range(size)])


def wide_tables(positions, yarn_divisor):
    angle_table = angles(positions, yarn_divisor)
    cosine, sine = jnp.cos(angle_table), jnp.sin(angle_table)
    return jnp.concatenate([cosine, cosine], axis=1), jnp.concatenate([-sine, sine], axis=1)


def rope_head(head, cosine, signed_sine):
    return head * cosine + pltpu.roll(head, HD // 2, 1) * signed_sine


def query_rope_kernel(head_order, query_ref, cosine_ref, sine_ref, out_ref):
    cosine, sine = cosine_ref[...], sine_ref[...]
    for place, head in enumerate(head_order):
        rows = query_ref[:, head * HD : (head + 1) * HD].astype(jnp.float32)
        out_ref[place] = rope_head(rows, cosine, sine).astype(jnp.bfloat16)


def terms_kernel(count, rows_ref, hidden_ref, *refs):
    out_ref = refs[-1]
    total = refs[count][...] if len(refs) > count + 1 else None
    for index, chunk_ref in enumerate(refs[:count]):
        depth = chunk_ref.shape[0]
        columns = pl.ds(pl.multiple_of(rows_ref[index], depth), depth)
        term = jnp.dot(hidden_ref[:, columns], chunk_ref[...], preferred_element_type=jnp.float32)
        total = term if total is None else total + term
    out_ref[...] = total


def pair_rope_kernel(block_ref, total_ref, hidden_ref, chunk_ref, cosine_ref, sine_ref, *refs):
    out_refs, sum_ref = refs[:-1], refs[-1]
    sum_ref[...] = total_ref[...] + jnp.dot(
        hidden_ref[...], chunk_ref[...], preferred_element_type=jnp.float32
    )
    cosine, sine = cosine_ref[...], sine_ref[...]
    for distance, out_ref in enumerate(out_refs):
        head = lax.rem(block_ref[0] + distance, len(out_refs))
        rows = sum_ref[:, pl.ds(pl.multiple_of(head * HD, HD), HD)]
        out_ref[...] = rope_head(rows, cosine, sine).astype(jnp.bfloat16)


def order_heads_kernel(head_order, block_ref, out_ref):
    for place, head in enumerate(head_order):
        out_ref[:, head * HD : (head + 1) * HD] = block_ref[place]


def attention_kernel(order_ref, place_ref, query_ref, *refs):
    spans = order_ref.shape[1]
    blocks = spans // 2
    mine_refs, theirs_refs = refs[:blocks], refs[blocks : 2 * blocks]
    out_ref, key_rows, value_rows = refs[2 * blocks :]
    sources, token_rows = query_ref.shape[1:3]
    per_span = sources // 2
    span_rows = per_span * token_rows
    place, block_here = place_ref[0], place_ref[1]
    keys_here = place % 2 == 0
    for distance in range(blocks):
        block = lax.rem(block_here + blocks - distance, blocks)
        for half in range(2):
            first = order_ref[0, 2 * block + half] * span_rows
            for part in range(per_span):
                slot = jnp.bitwise_xor(half * per_span + part, place)
                other = jnp.bitwise_xor(slot, 1)
                mine = mine_refs[distance][pl.ds(pl.multiple_of(slot * token_rows, token_rows), token_rows), :]
                theirs = theirs_refs[distance][
                    pl.ds(pl.multiple_of(other * token_rows, token_rows), token_rows), :
                ]
                rows = pl.ds(pl.multiple_of(first + part * token_rows, token_rows), token_rows)
                key_rows[rows, :] = jnp.where(keys_here, mine, theirs)
                value_rows[rows, :] = jnp.where(keys_here, theirs, mine)
    stored = []
    for position in range(spans):
        span = jnp.int32(0)
        for candidate in range(1, spans):
            span = jnp.where(order_ref[0, candidate] == position, candidate, span)
        stored.append((span // 2, span % 2))
    row_index = lax.broadcasted_iota(jnp.int32, (span_rows, span_rows), 0)
    column_index = lax.broadcasted_iota(jnp.int32, (span_rows, span_rows), 1)
    for position, (block, half) in enumerate(stored):
        query = query_ref[block, pl.ds(half * per_span, per_span)].reshape(span_rows, HD)
        reach = (position + 1) * span_rows
        score = tile_scores(query, key_rows[:reach, :])
        last = jnp.where(column_index <= row_index, score[:, position * span_rows :], -jnp.inf)
        score = jnp.concatenate([score[:, : position * span_rows], last], axis=1) if position else last
        row_top = jnp.max(score, axis=1, keepdims=True)
        weights = jnp.exp(score - row_top)
        denominator = jnp.sum(weights, axis=1, keepdims=True)
        numerator = jnp.dot(
            weights.astype(jnp.bfloat16), value_rows[:reach, :], preferred_element_type=jnp.float32
        )
        rows = (numerator / denominator).astype(jnp.bfloat16)
        out_ref[block, pl.ds(half * per_span, per_span)] = rows.reshape(per_span, token_rows, HD)


VMEM = pl.BlockSpec(memory_space=pltpu.VMEM)
SMEM = pl.BlockSpec(memory_space=pltpu.SMEM)


def whole_cycle_shards(hidden_in, queries, pair_weight, span_order, yarn_divisor):
    own_hidden = hidden_in[0]
    token_rows = own_hidden.shape[0]
    ulysses_size, cycle_size = lax.axis_size("ulysses"), lax.axis_size("blk")
    dp_size = lax.axis_size("dp")
    ulysses_index, cycle_index = lax.axis_index("ulysses"), lax.axis_index("blk")
    dp_index = lax.axis_index("dp")
    block_rows = token_rows * ulysses_size
    span_rows = block_rows // 2
    shard_rows = pair_weight.shape[0]
    kv_width = KVH * HD
    columns = cycle_size * HD
    core, chip = ulysses_index % 2, ulysses_index // 2

    piece = lax.dynamic_slice(
        pair_weight, (0, core * kv_width + chip * columns), (shard_rows, columns)
    )

    slot_devices = jnp.bitwise_xor(ulysses_index, jnp.arange(ulysses_size, dtype=jnp.int32))
    order_row = span_order[0]
    span_values = lax.dynamic_slice(order_row, (2 * cycle_index,), (2,))
    stored = slot_devices[:, None] * token_rows + jnp.arange(token_rows, dtype=jnp.int32)[None, :]
    stored = stored.reshape(block_rows)
    positions = jnp.where(stored < span_rows, span_values[0], span_values[1]) * span_rows + stored % span_rows
    cosine, sine = wide_tables(positions, yarn_divisor)
    own_cosine, own_sine = cosine[:token_rows], sine[:token_rows]
    pair_cosine = jnp.where(core == 0, cosine, 1.0)
    pair_sine = jnp.where(core == 0, sine, 0.0)

    head_order = [
        (chip_place * cycle_size + block) * 2 + core_place
        for block in range(cycle_size)
        for chip_place in range(ulysses_size // 2)
        for core_place in range(2)
    ]
    rotated = pl.pallas_call(
        lambda *refs: query_rope_kernel(head_order, *refs),
        out_shape=jax.ShapeDtypeStruct((QH, token_rows, HD), jnp.bfloat16),
        in_specs=[VMEM] * 3,
        out_specs=VMEM,
        compiler_params=pltpu.CompilerParams(vmem_limit_bytes=8 * 1024 * 1024),
        name="query_rope",
    )(queries[0], own_cosine, own_sine)
    def ahead(block, distance=1):
        return lax.ppermute(block, "blk", [(i, (i + distance) % cycle_size) for i in range(cycle_size)])

    def across(block):
        return lax.ppermute(block, "dp", [(i, dp_size - 1 - i) for i in range(dp_size)])

    def first_row(distance, row):
        return (row * cycle_size + jnp.remainder(cycle_index - distance, cycle_size)) * shard_rows

    other_row = dp_size - 1 - dp_index
    far_slots = [swap(own_hidden, distance) for distance in range(2, ulysses_size, 2)]
    partner = swap(own_hidden, 1)
    hidden = None

    def add_terms(chunks, total):
        before = [] if total is None else [total]
        return pl.pallas_call(
            functools.partial(terms_kernel, len(chunks)),
            out_shape=jax.ShapeDtypeStruct((block_rows, columns), jnp.float32),
            in_specs=[SMEM] + [VMEM] * (1 + len(chunks) + len(before)),
            out_specs=VMEM,
            compiler_params=pltpu.CompilerParams(vmem_limit_bytes=16 * 1024 * 1024),
            name="terms",
        )(jnp.stack([row for _, row in chunks]), hidden, *(chunk for chunk, _ in chunks), *before)

    travelling, crossed = piece, across(piece)
    received = [(piece, first_row(0, dp_index))]
    for distance in range(1, cycle_size - 1):
        travelling = ahead(travelling)
        if distance == 1:
            rotated, pair_cosine, pair_sine, travelling = lax.optimization_barrier(
                (rotated, pair_cosine, pair_sine, travelling)
            )
        travelling, crossed = lax.optimization_barrier((travelling, crossed))
        received += [
            (crossed, first_row(distance - 1, other_row)),
            (travelling, first_row(distance, dp_index)),
        ]
        crossed = across(travelling)

    *far_slots, travelling = lax.optimization_barrier((*far_slots, travelling))
    slots = [own_hidden, partner]
    for far in far_slots:
        slots += [far, swap(far, 1)]
    hidden = jnp.concatenate(slots, axis=0)
    total = add_terms(received, None)
    rotated, total = lax.optimization_barrier((rotated, total))
    query_rows = lax.all_to_all(rotated, ("blk", "ulysses"), split_axis=0, concat_axis=0, tiled=True)
    query_rows = query_rows.reshape(cycle_size, ulysses_size, token_rows, HD)

    travelling = ahead(travelling)
    travelling, crossed, total = lax.optimization_barrier((travelling, crossed, total))
    received = [
        (crossed, first_row(cycle_size - 2, other_row)),
        (travelling, first_row(cycle_size - 1, dp_index)),
    ]
    last_piece, last_row = across(travelling), first_row(cycle_size - 1, other_row)
    total = add_terms(received, total)
    last_hidden = lax.dynamic_slice(hidden, (0, last_row), (block_rows, shard_rows))
    last_piece, total, last_hidden = lax.optimization_barrier((last_piece, total, last_hidden))
    pairs = pl.pallas_call(
        pair_rope_kernel,
        out_shape=[jax.ShapeDtypeStruct((block_rows, HD), jnp.bfloat16)] * cycle_size,
        in_specs=[SMEM] + [VMEM] * 5,
        out_specs=[VMEM] * cycle_size,
        scratch_shapes=[pltpu.VMEM((block_rows, columns), jnp.float32)],
        compiler_params=pltpu.CompilerParams(vmem_limit_bytes=12 * 1024 * 1024),
        name="pair_rope",
    )(cycle_index.astype(jnp.int32).reshape(1), total, last_hidden, last_piece, pair_cosine, pair_sine)
    *pairs, query_rows = lax.optimization_barrier((*pairs, query_rows))
    mine, theirs = [pairs[0]] + [None] * (cycle_size - 1), [swap(pairs[0], 1)] + [None] * (cycle_size - 1)
    for distance in sorted(range(1, cycle_size), key=lambda d: -min(d, cycle_size - d)):
        mine[distance] = ahead(pairs[distance], distance)
        theirs[distance] = swap(mine[distance], 1)

    sequence_rows = cycle_size * block_rows
    attended = pl.pallas_call(
        attention_kernel,
        out_shape=jax.ShapeDtypeStruct((cycle_size, ulysses_size, token_rows, HD), jnp.bfloat16),
        in_specs=[SMEM, SMEM] + [VMEM] * (1 + 2 * cycle_size),
        out_specs=VMEM,
        scratch_shapes=[
            pltpu.VMEM((sequence_rows, HD), jnp.bfloat16),
            pltpu.VMEM((sequence_rows, HD), jnp.bfloat16),
        ],
        compiler_params=pltpu.CompilerParams(vmem_limit_bytes=24 * 1024 * 1024),
        name="attention",
    )(span_order, jnp.stack([ulysses_index, cycle_index]).astype(jnp.int32), query_rows, *mine, *theirs)
    heads = lax.all_to_all(
        attended.reshape(QH, token_rows, HD), ("blk", "ulysses"), split_axis=0, concat_axis=0, tiled=True
    )
    rows = pl.pallas_call(
        lambda *refs: order_heads_kernel(head_order, *refs),
        out_shape=jax.ShapeDtypeStruct((token_rows, QH * HD), jnp.bfloat16),
        in_specs=[VMEM],
        out_specs=VMEM,
        compiler_params=pltpu.CompilerParams(vmem_limit_bytes=8 * 1024 * 1024),
        name="order_heads",
    )(heads)
    return rows[None]


def solution(mesh):
    sizes = dict(mesh.shape)
    whole_cycle = (
        sizes["blk"] == STEPS + 1
        and sizes["ulysses"] * sizes["blk"] == QH
        and QH == 2 * KVH
        and sizes["ulysses"] & (sizes["ulysses"] - 1) == 0
        and sizes["dp"] == 2
    )
    return jax.shard_map(
        whole_cycle_shards if whole_cycle else general_shards,
        mesh=mesh,
        in_specs=(
            P("dp", ("blk", "ulysses"), None),
            P("dp", ("blk", "ulysses"), None),
            P(("dp", "blk"), None),
            P("dp", None),
            P(),
        ),
        out_specs=P("dp", ("blk", "ulysses"), None),
        check_vma=False,
    )
```

```python
import functools
import math

import jax
import jax.numpy as jnp
from jax import lax
from jax.experimental import pallas as pl
from jax.experimental.pallas import tpu as pltpu
from jax.sharding import Mesh
from jax.sharding import PartitionSpec as P

KVH = 8
HD = 128
QH = 16
STEPS = 3


LOG_BASE = math.log(500000.0)
LOG2_E = math.log2(math.e)


def from_behind(block, axis, distance):
    devices = range(lax.axis_size(axis))
    route = [((i - distance) % len(devices), i) for i in devices]
    return lax.ppermute(block, axis, route)


def rotate(vectors, angle_table):
    half_dim = vectors.shape[-1] // 2
    first_half = vectors[..., :half_dim]
    second_half = vectors[..., half_dim:]
    cosine = jnp.cos(angle_table)
    sine_part = jnp.sin(angle_table)
    return jnp.concatenate(
        [
            first_half * cosine - second_half * sine_part,
            second_half * cosine + first_half * sine_part,
        ],
        axis=-1,
    )


def angles(positions, yarn_divisor):
    half_dim = yarn_divisor.shape[0]
    scaled = 2.0 * jnp.arange(half_dim, dtype=jnp.float32) / (2 * half_dim)
    inverse = jnp.exp(-LOG_BASE * scaled) / yarn_divisor.astype(jnp.float32)
    return positions.astype(jnp.float32)[:, None] * inverse[None, :]


def positions_of(order_row, first_row, row_count, span_rows):
    stored = first_row + jnp.arange(row_count, dtype=jnp.int32)
    span_index = stored // span_rows
    matches = span_index[:, None] == jnp.arange(order_row.shape[0], dtype=jnp.int32)[None, :]
    span_value = jnp.sum(jnp.where(matches, order_row[None, :], 0), axis=1)
    return span_value * span_rows + stored % span_rows


def tile_scores(query_rows, key_rows):
    product = lax.dot_general(
        query_rows, key_rows, (((1,), (1,)), ((), ())), preferred_element_type=jnp.float32
    )
    return product * (1.0 / math.sqrt(HD))


def row_maximum(query_rows, query_pos, key_rows, key_pos):
    score = tile_scores(query_rows, key_rows)
    return jnp.max(jnp.where(key_pos[None, :] <= query_pos[:, None], score, -jnp.inf), axis=1)


def add_tile(denominator, numerator, query_rows, query_pos, key_rows, value_rows, key_pos, row_top):
    score = tile_scores(query_rows, key_rows)
    allowed = key_pos[None, :] <= query_pos[:, None]
    weights = jnp.where(allowed, jnp.exp(score - row_top[:, None]), 0.0)
    denominator = denominator + jnp.sum(weights, axis=1)
    numerator = numerator + jnp.dot(
        weights.astype(jnp.bfloat16), value_rows, preferred_element_type=jnp.float32
    )
    return (denominator, numerator)


def general_shards(hidden_in, queries, pair_weight, span_order, yarn_divisor):
    inputs_local = hidden_in[0]
    queries_local = queries[0]
    order_row = span_order[0]
    token_rows = inputs_local.shape[0]
    ulysses_size = lax.axis_size("ulysses")
    cycle_size = lax.axis_size("blk")
    ulysses_index = lax.axis_index("ulysses")
    cycle_index = lax.axis_index("blk")
    block_rows = token_rows * ulysses_size
    span_rows = block_rows // 2
    kv_width = KVH * HD
    kv_local = KVH // ulysses_size
    group_size = QH // KVH
    own_positions = positions_of(
        order_row, cycle_index * block_rows + ulysses_index * token_rows, token_rows, span_rows
    )
    own_angles = angles(own_positions, yarn_divisor)
    block_positions = positions_of(order_row, cycle_index * block_rows, block_rows, span_rows)
    rotated_queries = rotate(
        queries_local.astype(jnp.float32).reshape(token_rows, QH, HD), own_angles[:, None, :]
    )
    rotated_queries = rotated_queries.astype(jnp.bfloat16).reshape(token_rows, QH * HD)
    projected = jnp.dot(
        inputs_local,
        lax.all_gather(pair_weight, ("dp", "blk"), axis=0, tiled=True),
        preferred_element_type=jnp.float32,
    )
    token_keys = rotate(
        projected[:, :kv_width].reshape(token_rows, KVH, HD), own_angles[:, None, :]
    )
    token_keys = token_keys.astype(jnp.bfloat16).reshape(token_rows, kv_width)
    token_values = projected[:, kv_width:].astype(jnp.bfloat16)
    query_block, key_block, value_block = (
        lax.all_to_all(rotated_queries, "ulysses", split_axis=1, concat_axis=0, tiled=True),
        lax.all_to_all(token_keys, "ulysses", split_axis=1, concat_axis=0, tiled=True),
        lax.all_to_all(token_values, "ulysses", split_axis=1, concat_axis=0, tiled=True),
    )
    own_pair = jnp.stack([key_block, value_block])
    carried_blocks = [own_pair]
    current_pair = own_pair
    for step_index in range(STEPS):
        current_pair = from_behind(current_pair, "blk", 1)
        carried_blocks.append(current_pair)
    carried_positions = []
    for step_index in range(STEPS + 1):
        source_block = jnp.remainder(cycle_index - step_index, cycle_size)
        carried_positions.append(
            positions_of(order_row, source_block * block_rows, block_rows, span_rows)
        )
    output_rows = []
    for query_half in range(2):
        row_start = query_half * span_rows
        half_positions = block_positions[row_start : row_start + span_rows]
        query_pos = jnp.tile(half_positions, group_size)
        head_outputs = []
        for local_head in range(kv_local):
            query_part = query_block[
                row_start : row_start + span_rows,
                local_head * group_size * HD : (local_head + 1) * group_size * HD,
            ]
            query_rows = (
                query_part.reshape(span_rows, group_size, HD)
                .transpose(1, 0, 2)
                .reshape(group_size * span_rows, HD)
            )
            tile_list = []
            for step_index in range(STEPS + 1):
                pair_block = carried_blocks[step_index]
                for key_half in range(2):
                    key_start = key_half * span_rows
                    key_rows = pair_block[
                        0,
                        key_start : key_start + span_rows,
                        local_head * HD : (local_head + 1) * HD,
                    ]
                    value_rows = pair_block[
                        1,
                        key_start : key_start + span_rows,
                        local_head * HD : (local_head + 1) * HD,
                    ]
                    key_pos = carried_positions[step_index][key_start : key_start + span_rows]
                    tile_list.append((key_rows, value_rows, key_pos))
            row_top = jnp.full((group_size * span_rows,), -jnp.inf, jnp.float32)
            for key_rows, value_rows, key_pos in tile_list:
                tile_top = row_maximum(query_rows, query_pos, key_rows, key_pos)
                row_top = jnp.maximum(row_top, tile_top)
            denominator = jnp.zeros((group_size * span_rows,), jnp.float32)
            numerator = jnp.zeros((group_size * span_rows, HD), jnp.float32)
            for key_rows, value_rows, key_pos in tile_list:
                denominator, numerator = add_tile(
                    denominator,
                    numerator,
                    query_rows,
                    query_pos,
                    key_rows,
                    value_rows,
                    key_pos,
                    row_top,
                )
            normalized = (numerator / denominator[:, None]).astype(jnp.bfloat16)
            normalized = (
                normalized.reshape(group_size, span_rows, HD)
                .transpose(1, 0, 2)
                .reshape(span_rows, group_size * HD)
            )
            head_outputs.append(normalized)
        output_rows.append(jnp.concatenate(head_outputs, axis=1))
    block_output = jnp.concatenate(output_rows, axis=0)
    token_output = lax.all_to_all(block_output, "ulysses", split_axis=0, concat_axis=1, tiled=True)
    return token_output[None]


def exchange(block, axis, distance):
    size = lax.axis_size(axis)
    return lax.ppermute(block, axis, [(i, i ^ distance) for i in range(size)])


def wide_tables(positions, yarn_divisor):
    angle_table = angles(positions, yarn_divisor)
    cosine, sine = jnp.cos(angle_table), jnp.sin(angle_table)
    return jnp.concatenate([cosine, cosine], axis=1), jnp.concatenate([-sine, sine], axis=1)


def rope_head(head, cosine, signed_sine):
    return head * cosine + pltpu.roll(head, HD // 2, 1) * signed_sine


def query_rope_kernel(pair_order, query_ref, cosine_ref, sine_ref, out_ref):
    cosine, sine = cosine_ref[...], sine_ref[...]
    width = out_ref.shape[2]
    for place, pair in enumerate(pair_order):
        for start in range(0, width, HD):
            column = pair * width + start
            rows = query_ref[:, column : column + HD].astype(jnp.float32)
            out_ref[place, :, start : start + HD] = rope_head(rows, cosine, sine).astype(jnp.bfloat16)


def load_terms(rows_ref, slot_refs, piece_refs, hidden_rows, pieces, sems):
    token_rows = slot_refs[0].shape[0]
    copies = []
    for index, piece_ref in enumerate(piece_refs):
        depth = piece_ref.shape[0]
        columns = pl.ds(pl.multiple_of(rows_ref[index], depth), depth)
        started = [pltpu.make_async_copy(piece_ref, pieces.at[index], sems.at[index, 0])]
        for slot, slot_ref in enumerate(slot_refs):
            rows = hidden_rows.at[index, pl.ds(slot * token_rows, token_rows)]
            started.append(pltpu.make_async_copy(slot_ref.at[:, columns], rows, sems.at[index, slot + 1]))
        for copy in started:
            copy.start()
        copies.append(started)
    return copies


def terms_kernel(slots, count, rows_ref, *refs):
    slot_refs, piece_refs = refs[:slots], refs[slots : slots + count]
    out_ref, next_hidden_ref, hidden_rows, pieces, sems, next_sems = refs[slots + count :]
    copies = load_terms(rows_ref, slot_refs, piece_refs, hidden_rows, pieces, sems)
    token_rows, depth = slot_refs[0].shape[0], piece_refs[0].shape[0]
    columns = pl.ds(pl.multiple_of(rows_ref[count], depth), depth)
    next_copies = [
        pltpu.make_async_copy(
            slot_ref.at[:, columns],
            next_hidden_ref.at[pl.ds(slot * token_rows, token_rows)],
            next_sems.at[slot],
        )
        for slot, slot_ref in enumerate(slot_refs)
    ]
    for copy in next_copies:
        copy.start()
    total = None
    for index, started in enumerate(copies):
        for copy in started:
            copy.wait()
        term = jnp.dot(hidden_rows[index], pieces[index], preferred_element_type=jnp.float32)
        total = term if total is None else total + term
    out_ref[...] = total
    for copy in next_copies:
        copy.wait()


def pair_rope_kernel(place_ref, total_ref, hidden_ref, piece_ref, cosine_ref, sine_ref, *refs):
    out_refs, sum_ref = refs[:-1], refs[-1]
    sum_ref[...] = total_ref[...] + jnp.dot(
        hidden_ref[...], piece_ref[...], preferred_element_type=jnp.float32
    )
    cosine, sine = cosine_ref[...], sine_ref[...]
    for distance, out_ref in enumerate(out_refs):
        head = lax.rem(place_ref[1] + distance, len(out_refs))
        rows = sum_ref[:, pl.ds(pl.multiple_of(head * HD, HD), HD)]
        out_ref[...] = rope_head(rows, cosine, sine).astype(jnp.bfloat16)


def order_heads_kernel(place_ref, *refs):
    out_ref = refs[-1]
    blocks = (len(refs) - 1) // 2
    chip, block_here = place_ref[0] // 2, place_ref[1]
    width = refs[0].shape[-1]
    for distance in range(blocks):
        block = lax.rem(block_here + blocks - distance, blocks)
        near, far = refs[distance], refs[blocks + distance]
        for source, rows in ((chip, near[...] if distance == 0 else near[0]), (1 - chip, far[...])):
            pair = source * blocks + block
            out_ref[:, pl.ds(pl.multiple_of(pair * width, width), width)] = rows


def attention_kernel(order_ref, place_ref, query_ref, *refs):
    spans = order_ref.shape[1]
    blocks = spans // 2
    mine_refs, theirs_refs = refs[:blocks], refs[blocks : 2 * blocks]
    near_ref, far_ref, *both_refs = refs[2 * blocks : 3 * blocks + 1]
    key_rows, value_rows, out_rows = refs[3 * blocks + 1 :]
    token_rows = query_ref.shape[1]
    span_rows = 2 * token_rows
    place, block_here = place_ref[0], place_ref[1]
    chip, core = place // 2, place % 2
    for distance in range(blocks):
        block = lax.rem(block_here + blocks - distance, blocks)
        for half in range(2):
            first = order_ref[0, 2 * block + half] * span_rows
            for part in range(2):
                slot = jnp.bitwise_xor(half * 2 + part, place)
                other = jnp.bitwise_xor(slot, 1)
                mine = mine_refs[distance][pl.ds(pl.multiple_of(slot * token_rows, token_rows), token_rows), :]
                theirs = theirs_refs[distance][
                    pl.ds(pl.multiple_of(other * token_rows, token_rows), token_rows), :
                ]
                rows = pl.ds(pl.multiple_of(first + part * token_rows, token_rows), token_rows)
                key_rows[rows, :] = jnp.where(core == 0, mine, theirs)
                value_rows[rows, :] = jnp.where(core == 0, theirs, mine)
    stored = []
    for position in range(spans):
        span = jnp.int32(0)
        for candidate in range(1, spans):
            span = jnp.where(order_ref[0, candidate] == position, candidate, span)
        stored.append(span)
    square = (2 * token_rows, span_rows)
    row_index = lax.broadcasted_iota(jnp.int32, square, 0) % token_rows + core * token_rows
    allowed = lax.broadcasted_iota(jnp.int32, square, 1) <= row_index

    def scores(position):
        pair = query_ref[stored[position]]
        query = jnp.concatenate([pair[:, :HD], pair[:, HD:]], axis=0)
        score = lax.dot_general(
            query,
            key_rows[: (position + 1) * span_rows, :],
            (((1,), (1,)), ((), ())),
            preferred_element_type=jnp.float32,
        )
        start = position * span_rows
        last = jnp.where(allowed, score[:, start:], -jnp.inf)
        return jnp.concatenate([score[:, :start], last], axis=1) if position else last

    score = scores(spans - 1)
    for position in reversed(range(spans)):
        following = scores(position - 1) if position else None
        row_top = jnp.max(score, axis=1, keepdims=True)
        weights = jnp.exp2((score - row_top) * (LOG2_E / math.sqrt(HD)))
        denominator = jnp.sum(weights, axis=1, keepdims=True)
        numerator = jnp.dot(
            weights.astype(jnp.bfloat16),
            value_rows[: (position + 1) * span_rows, :],
            preferred_element_type=jnp.float32,
        )
        rows = (numerator / denominator).astype(jnp.bfloat16)
        out_rows[stored[position]] = jnp.concatenate([rows[:token_rows], rows[token_rows:]], axis=1)
        score = following
    near_ref[...] = out_rows[2 * block_here + chip]
    far_ref[...] = out_rows[2 * block_here + 1 - chip]
    for distance, both_ref in enumerate(both_refs, 1):
        block = lax.rem(block_here + distance, blocks)
        both_ref[0] = out_rows[2 * block + chip]
        both_ref[1] = out_rows[2 * block + 1 - chip]


VMEM = pl.BlockSpec(memory_space=pltpu.VMEM)
ANY = pl.BlockSpec(memory_space=pl.ANY)
SMEM = pl.BlockSpec(memory_space=pltpu.SMEM)


def whole_cycle_shards(hidden_in, queries, pair_weight, span_order, yarn_divisor):
    own_hidden = hidden_in[0]
    token_rows = own_hidden.shape[0]
    ulysses_size, cycle_size = 2 * lax.axis_size("chip"), lax.axis_size("blk")
    dp_size = lax.axis_size("dp")
    chip, core = lax.axis_index("chip"), lax.axis_index("core")
    ulysses_index, cycle_index = 2 * chip + core, lax.axis_index("blk")
    dp_index = lax.axis_index("dp")
    block_rows = token_rows * ulysses_size
    span_rows = block_rows // 2
    shard_rows = pair_weight.shape[0]
    kv_width = KVH * HD
    columns = cycle_size * HD

    piece = lax.dynamic_slice(
        pair_weight, (0, core * kv_width + chip * columns), (shard_rows, columns)
    )

    slot_devices = jnp.bitwise_xor(ulysses_index, jnp.arange(ulysses_size, dtype=jnp.int32))
    order_row = span_order[0]
    span_values = lax.dynamic_slice(order_row, (2 * cycle_index,), (2,))
    stored = slot_devices[:, None] * token_rows + jnp.arange(token_rows, dtype=jnp.int32)[None, :]
    stored = stored.reshape(block_rows)
    positions = jnp.where(stored < span_rows, span_values[0], span_values[1]) * span_rows + stored % span_rows
    cosine, sine = wide_tables(positions, yarn_divisor)
    own_cosine, own_sine = cosine[:token_rows], sine[:token_rows]
    pair_cosine = jnp.where(core == 0, cosine, 1.0)
    pair_sine = jnp.where(core == 0, sine, 0.0)

    pair_order = [
        place * cycle_size + block for block in range(cycle_size) for place in range(ulysses_size // 2)
    ]
    rotated = pl.pallas_call(
        functools.partial(query_rope_kernel, pair_order),
        out_shape=jax.ShapeDtypeStruct((len(pair_order), token_rows, 2 * HD), jnp.bfloat16),
        in_specs=[VMEM] * 3,
        out_specs=VMEM,
        compiler_params=pltpu.CompilerParams(vmem_limit_bytes=8 * 1024 * 1024),
        name="query_rope",
    )(queries[0], own_cosine, own_sine)

    def ahead(block, distance=1):
        return lax.ppermute(block, "blk", [(i, (i + distance) % cycle_size) for i in range(cycle_size)])

    def across(block):
        return lax.ppermute(block, "dp", [(i, dp_size - 1 - i) for i in range(dp_size)])

    def first_row(distance, row):
        return (row * cycle_size + jnp.remainder(cycle_index - distance, cycle_size)) * shard_rows

    other_row = dp_size - 1 - dp_index
    far = exchange(own_hidden, "chip", 1)
    partner = exchange(own_hidden, "core", 1)

    travelling, crossed = piece, across(piece)
    received = [piece]
    firsts = [first_row(0, dp_index)]
    for distance in range(1, cycle_size):
        firsts += [first_row(distance - 1, other_row), first_row(distance, dp_index)]
    rows = jnp.stack([*firsts, first_row(cycle_size - 1, other_row)])
    place = jnp.stack([ulysses_index, cycle_index]).astype(jnp.int32)
    for distance in range(1, cycle_size - 1):
        travelling = ahead(travelling)
        if distance == 1:
            rotated, pair_cosine, pair_sine, rows, place, travelling = lax.optimization_barrier(
                (rotated, pair_cosine, pair_sine, rows, place, travelling)
            )
        travelling, crossed = lax.optimization_barrier((travelling, crossed))
        received += [crossed, travelling]
        crossed = across(travelling)

    far, travelling = lax.optimization_barrier((far, travelling))
    hidden = [own_hidden, partner, far, exchange(far, "core", 1)]
    *hidden, rotated = lax.optimization_barrier((*hidden, rotated))
    query_rows = lax.all_to_all(rotated, ("blk", "chip"), split_axis=0, concat_axis=0, tiled=True)

    travelling = ahead(travelling)
    travelling, crossed = lax.optimization_barrier((travelling, crossed))
    received += [crossed, travelling]
    last_piece = across(travelling)
    total, last_hidden = pl.pallas_call(
        functools.partial(terms_kernel, ulysses_size, len(received)),
        out_shape=[
            jax.ShapeDtypeStruct((block_rows, columns), jnp.float32),
            jax.ShapeDtypeStruct((block_rows, shard_rows), jnp.bfloat16),
        ],
        in_specs=[SMEM] + [ANY] * (ulysses_size + len(received)),
        out_specs=[VMEM] * 2,
        scratch_shapes=[
            pltpu.VMEM((len(received), block_rows, shard_rows), jnp.bfloat16),
            pltpu.VMEM((len(received), shard_rows, columns), jnp.bfloat16),
            pltpu.SemaphoreType.DMA((len(received), ulysses_size + 1)),
            pltpu.SemaphoreType.DMA((ulysses_size,)),
        ],
        compiler_params=pltpu.CompilerParams(vmem_limit_bytes=20 * 1024 * 1024),
        name="terms",
    )(rows, *hidden, *received)
    last_piece, total, last_hidden = lax.optimization_barrier((last_piece, total, last_hidden))
    pairs = pl.pallas_call(
        pair_rope_kernel,
        out_shape=[jax.ShapeDtypeStruct((block_rows, HD), jnp.bfloat16)] * cycle_size,
        in_specs=[SMEM] + [VMEM] * 5,
        out_specs=[VMEM] * cycle_size,
        scratch_shapes=[pltpu.VMEM((block_rows, columns), jnp.float32)],
        compiler_params=pltpu.CompilerParams(vmem_limit_bytes=12 * 1024 * 1024),
        name="pair_rope",
    )(place, total, last_hidden, last_piece, pair_cosine, pair_sine)
    *pairs, query_rows = lax.optimization_barrier((*pairs, query_rows))
    far_first = sorted(range(1, cycle_size), key=lambda distance: -min(distance, cycle_size - distance))
    mine, theirs = {0: pairs[0]}, {0: exchange(pairs[0], "core", 1)}
    for distance in far_first:
        mine[distance] = ahead(pairs[distance], distance)
        theirs[distance] = exchange(mine[distance], "core", 1)
    in_order = range(cycle_size)

    sequence_rows = cycle_size * block_rows
    one = jax.ShapeDtypeStruct((token_rows, 2 * HD), jnp.bfloat16)
    both = jax.ShapeDtypeStruct((2, token_rows, 2 * HD), jnp.bfloat16)
    near, far, *rest = pl.pallas_call(
        attention_kernel,
        out_shape=[one, one] + [both] * (cycle_size - 1),
        in_specs=[SMEM, SMEM] + [VMEM] * (1 + 2 * cycle_size),
        out_specs=[VMEM] * (cycle_size + 1),
        scratch_shapes=[
            pltpu.VMEM((sequence_rows, HD), jnp.bfloat16),
            pltpu.VMEM((sequence_rows, HD), jnp.bfloat16),
            pltpu.VMEM((len(pair_order), token_rows, 2 * HD), jnp.bfloat16),
        ],
        compiler_params=pltpu.CompilerParams(vmem_limit_bytes=24 * 1024 * 1024),
        name="attention",
    )(span_order, place, query_rows, *(mine[d] for d in in_order), *(theirs[d] for d in in_order))
    arrived = {distance: ahead(rest[distance - 1], distance) for distance in far_first}
    crossed = {0: exchange(far, "chip", 1)}
    for distance in far_first:
        crossed[distance] = exchange(arrived[distance][1], "chip", 1)
    arrived[0] = near
    heads = pl.pallas_call(
        order_heads_kernel,
        out_shape=jax.ShapeDtypeStruct((token_rows, QH * HD), jnp.bfloat16),
        in_specs=[SMEM] + [VMEM] * (2 * cycle_size),
        out_specs=VMEM,
        compiler_params=pltpu.CompilerParams(vmem_limit_bytes=8 * 1024 * 1024),
        name="order_heads",
    )(place, *(arrived[d] for d in in_order), *(crossed[d] for d in in_order))
    return heads[None]


def solution(mesh):
    sizes = dict(mesh.shape)
    specs = dict(
        in_specs=(
            P("dp", ("blk", "ulysses"), None),
            P("dp", ("blk", "ulysses"), None),
            P(("dp", "blk"), None),
            P("dp", None),
            P(),
        ),
        out_specs=P("dp", ("blk", "ulysses"), None),
        check_vma=False,
    )
    whole_cycle = (
        sizes["blk"] == STEPS + 1
        and sizes["ulysses"] == 4
        and sizes["dp"] == 2
        and sizes["ulysses"] * sizes["blk"] == QH == 2 * KVH
    )
    if not whole_cycle:
        return jax.shard_map(general_shards, mesh=mesh, **specs)
    chips = Mesh(
        mesh.devices.reshape(sizes["dp"], sizes["ulysses"] // 2, 2, sizes["blk"]),
        ("dp", "chip", "core", "blk"),
    )
    rows = P("dp", ("blk", "chip", "core"), None)
    specs["in_specs"] = (rows, rows, *specs["in_specs"][2:])
    specs["out_specs"] = rows
    return jax.shard_map(whole_cycle_shards, mesh=chips, **specs)
```

```python
import functools
import math

import jax
import jax.numpy as jnp
from jax import lax
from jax.experimental import pallas as pl
from jax.experimental.pallas import tpu as pltpu
from jax.sharding import Mesh
from jax.sharding import PartitionSpec as P

KVH = 8
HD = 128
QH = 16
STEPS = 3


LOG_BASE = math.log(500000.0)
LOG2_E = math.log2(math.e)


def from_behind(block, axis, distance):
    devices = range(lax.axis_size(axis))
    route = [((i - distance) % len(devices), i) for i in devices]
    return lax.ppermute(block, axis, route)


def rotate(vectors, angle_table):
    half_dim = vectors.shape[-1] // 2
    first_half = vectors[..., :half_dim]
    second_half = vectors[..., half_dim:]
    cosine = jnp.cos(angle_table)
    sine_part = jnp.sin(angle_table)
    return jnp.concatenate(
        [
            first_half * cosine - second_half * sine_part,
            second_half * cosine + first_half * sine_part,
        ],
        axis=-1,
    )


def angles(positions, yarn_divisor):
    half_dim = yarn_divisor.shape[0]
    scaled = 2.0 * jnp.arange(half_dim, dtype=jnp.float32) / (2 * half_dim)
    inverse = jnp.exp(-LOG_BASE * scaled) / yarn_divisor.astype(jnp.float32)
    return positions.astype(jnp.float32)[:, None] * inverse[None, :]


def positions_of(order_row, first_row, row_count, span_rows):
    stored = first_row + jnp.arange(row_count, dtype=jnp.int32)
    span_index = stored // span_rows
    matches = span_index[:, None] == jnp.arange(order_row.shape[0], dtype=jnp.int32)[None, :]
    span_value = jnp.sum(jnp.where(matches, order_row[None, :], 0), axis=1)
    return span_value * span_rows + stored % span_rows


def tile_scores(query_rows, key_rows):
    product = lax.dot_general(
        query_rows, key_rows, (((1,), (1,)), ((), ())), preferred_element_type=jnp.float32
    )
    return product * (1.0 / math.sqrt(HD))


def row_maximum(query_rows, query_pos, key_rows, key_pos):
    score = tile_scores(query_rows, key_rows)
    return jnp.max(jnp.where(key_pos[None, :] <= query_pos[:, None], score, -jnp.inf), axis=1)


def add_tile(denominator, numerator, query_rows, query_pos, key_rows, value_rows, key_pos, row_top):
    score = tile_scores(query_rows, key_rows)
    allowed = key_pos[None, :] <= query_pos[:, None]
    weights = jnp.where(allowed, jnp.exp(score - row_top[:, None]), 0.0)
    denominator = denominator + jnp.sum(weights, axis=1)
    numerator = numerator + jnp.dot(
        weights.astype(jnp.bfloat16), value_rows, preferred_element_type=jnp.float32
    )
    return (denominator, numerator)


def general_shards(hidden_in, queries, pair_weight, span_order, yarn_divisor):
    inputs_local = hidden_in[0]
    queries_local = queries[0]
    order_row = span_order[0]
    token_rows = inputs_local.shape[0]
    ulysses_size = lax.axis_size("ulysses")
    cycle_size = lax.axis_size("blk")
    ulysses_index = lax.axis_index("ulysses")
    cycle_index = lax.axis_index("blk")
    block_rows = token_rows * ulysses_size
    span_rows = block_rows // 2
    kv_width = KVH * HD
    kv_local = KVH // ulysses_size
    group_size = QH // KVH
    own_positions = positions_of(
        order_row, cycle_index * block_rows + ulysses_index * token_rows, token_rows, span_rows
    )
    own_angles = angles(own_positions, yarn_divisor)
    block_positions = positions_of(order_row, cycle_index * block_rows, block_rows, span_rows)
    rotated_queries = rotate(
        queries_local.astype(jnp.float32).reshape(token_rows, QH, HD), own_angles[:, None, :]
    )
    rotated_queries = rotated_queries.astype(jnp.bfloat16).reshape(token_rows, QH * HD)
    projected = jnp.dot(
        inputs_local,
        lax.all_gather(pair_weight, ("dp", "blk"), axis=0, tiled=True),
        preferred_element_type=jnp.float32,
    )
    token_keys = rotate(
        projected[:, :kv_width].reshape(token_rows, KVH, HD), own_angles[:, None, :]
    )
    token_keys = token_keys.astype(jnp.bfloat16).reshape(token_rows, kv_width)
    token_values = projected[:, kv_width:].astype(jnp.bfloat16)
    query_block, key_block, value_block = (
        lax.all_to_all(rotated_queries, "ulysses", split_axis=1, concat_axis=0, tiled=True),
        lax.all_to_all(token_keys, "ulysses", split_axis=1, concat_axis=0, tiled=True),
        lax.all_to_all(token_values, "ulysses", split_axis=1, concat_axis=0, tiled=True),
    )
    own_pair = jnp.stack([key_block, value_block])
    carried_blocks = [own_pair]
    current_pair = own_pair
    for step_index in range(STEPS):
        current_pair = from_behind(current_pair, "blk", 1)
        carried_blocks.append(current_pair)
    carried_positions = []
    for step_index in range(STEPS + 1):
        source_block = jnp.remainder(cycle_index - step_index, cycle_size)
        carried_positions.append(
            positions_of(order_row, source_block * block_rows, block_rows, span_rows)
        )
    output_rows = []
    for query_half in range(2):
        row_start = query_half * span_rows
        half_positions = block_positions[row_start : row_start + span_rows]
        query_pos = jnp.tile(half_positions, group_size)
        head_outputs = []
        for local_head in range(kv_local):
            query_part = query_block[
                row_start : row_start + span_rows,
                local_head * group_size * HD : (local_head + 1) * group_size * HD,
            ]
            query_rows = (
                query_part.reshape(span_rows, group_size, HD)
                .transpose(1, 0, 2)
                .reshape(group_size * span_rows, HD)
            )
            tile_list = []
            for step_index in range(STEPS + 1):
                pair_block = carried_blocks[step_index]
                for key_half in range(2):
                    key_start = key_half * span_rows
                    key_rows = pair_block[
                        0,
                        key_start : key_start + span_rows,
                        local_head * HD : (local_head + 1) * HD,
                    ]
                    value_rows = pair_block[
                        1,
                        key_start : key_start + span_rows,
                        local_head * HD : (local_head + 1) * HD,
                    ]
                    key_pos = carried_positions[step_index][key_start : key_start + span_rows]
                    tile_list.append((key_rows, value_rows, key_pos))
            row_top = jnp.full((group_size * span_rows,), -jnp.inf, jnp.float32)
            for key_rows, value_rows, key_pos in tile_list:
                tile_top = row_maximum(query_rows, query_pos, key_rows, key_pos)
                row_top = jnp.maximum(row_top, tile_top)
            denominator = jnp.zeros((group_size * span_rows,), jnp.float32)
            numerator = jnp.zeros((group_size * span_rows, HD), jnp.float32)
            for key_rows, value_rows, key_pos in tile_list:
                denominator, numerator = add_tile(
                    denominator,
                    numerator,
                    query_rows,
                    query_pos,
                    key_rows,
                    value_rows,
                    key_pos,
                    row_top,
                )
            normalized = (numerator / denominator[:, None]).astype(jnp.bfloat16)
            normalized = (
                normalized.reshape(group_size, span_rows, HD)
                .transpose(1, 0, 2)
                .reshape(span_rows, group_size * HD)
            )
            head_outputs.append(normalized)
        output_rows.append(jnp.concatenate(head_outputs, axis=1))
    block_output = jnp.concatenate(output_rows, axis=0)
    token_output = lax.all_to_all(block_output, "ulysses", split_axis=0, concat_axis=1, tiled=True)
    return token_output[None]


def far_first(size):
    return sorted(range(1, size), key=lambda distance: -min(distance, size - distance))


def exchange(block, axis, distance):
    size = lax.axis_size(axis)
    return lax.ppermute(block, axis, [(i, i ^ distance) for i in range(size)])


def wide_tables(positions, yarn_divisor):
    angle_table = angles(positions, yarn_divisor)
    cosine, sine = jnp.cos(angle_table), jnp.sin(angle_table)
    return jnp.concatenate([cosine, cosine], axis=1), jnp.concatenate([-sine, sine], axis=1)


def rope_head(head, cosine, signed_sine):
    return head * cosine + pltpu.roll(head, HD // 2, 1) * signed_sine


def query_rope_kernel(place_ref, query_ref, cosine_ref, sine_ref, far_ref, *near_refs):
    cosine, sine = cosine_ref[...], sine_ref[...]
    blocks, width = far_ref.shape[0], far_ref.shape[2]
    chip, block_here = place_ref[0] // 2, place_ref[1]
    for distance, near_ref in enumerate(near_refs):
        block = lax.rem(block_here + distance, blocks)
        for target, out_ref in ((chip, near_ref), (1 - chip, far_ref.at[distance])):
            columns = pl.ds(pl.multiple_of((target * blocks + block) * width, width), width)
            pair = query_ref[:, columns].astype(jnp.float32)
            for start in range(0, width, HD):
                rows = rope_head(pair[:, start : start + HD], cosine, sine)
                out_ref[:, start : start + HD] = rows.astype(jnp.bfloat16)


def pack_kernel(far_ref, *refs):
    near_refs, out_refs = refs[: len(refs) // 2], refs[len(refs) // 2 :]
    for distance, (near_ref, out_ref) in enumerate(zip(near_refs, out_refs), 1):
        out_ref[0] = near_ref[...]
        out_ref[1] = far_ref[distance]


def load_terms(rows_ref, slot_refs, piece_refs, hidden_rows, pieces, sems):
    token_rows = slot_refs[0].shape[0]
    copies = []
    for index, piece_ref in enumerate(piece_refs):
        depth = piece_ref.shape[0]
        columns = pl.ds(pl.multiple_of(rows_ref[index], depth), depth)
        started = [pltpu.make_async_copy(piece_ref, pieces.at[index], sems.at[index, 0])]
        for slot, slot_ref in enumerate(slot_refs):
            rows = hidden_rows.at[index, pl.ds(slot * token_rows, token_rows)]
            started.append(pltpu.make_async_copy(slot_ref.at[:, columns], rows, sems.at[index, slot + 1]))
        for copy in started:
            copy.start()
        copies.append(started)
    return copies


def terms_kernel(slots, count, rows_ref, *refs):
    slot_refs, piece_refs = refs[:slots], refs[slots : slots + count]
    out_ref, next_hidden_ref, hidden_rows, pieces, sems, next_sems = refs[slots + count :]
    copies = load_terms(rows_ref, slot_refs, piece_refs, hidden_rows, pieces, sems)
    token_rows, depth = slot_refs[0].shape[0], piece_refs[0].shape[0]
    columns = pl.ds(pl.multiple_of(rows_ref[count], depth), depth)
    next_copies = [
        pltpu.make_async_copy(
            slot_ref.at[:, columns],
            next_hidden_ref.at[pl.ds(slot * token_rows, token_rows)],
            next_sems.at[slot],
        )
        for slot, slot_ref in enumerate(slot_refs)
    ]
    for copy in next_copies:
        copy.start()
    total = None
    for index, started in enumerate(copies):
        for copy in started:
            copy.wait()
        term = jnp.dot(hidden_rows[index], pieces[index], preferred_element_type=jnp.float32)
        total = term if total is None else total + term
    out_ref[...] = total
    for copy in next_copies:
        copy.wait()


def pair_rope_kernel(place_ref, total_ref, hidden_ref, piece_ref, cosine_ref, sine_ref, *refs):
    out_refs, sum_ref = refs[:-1], refs[-1]
    sum_ref[...] = total_ref[...] + jnp.dot(
        hidden_ref[...], piece_ref[...], preferred_element_type=jnp.float32
    )
    cosine, sine = cosine_ref[...], sine_ref[...]
    for distance, out_ref in enumerate(out_refs):
        head = lax.rem(place_ref[1] + distance, len(out_refs))
        rows = sum_ref[:, pl.ds(pl.multiple_of(head * HD, HD), HD)]
        out_ref[...] = rope_head(rows, cosine, sine).astype(jnp.bfloat16)


def order_heads_kernel(place_ref, *refs):
    out_ref = refs[-1]
    blocks = (len(refs) - 1) // 2
    chip, block_here = place_ref[0] // 2, place_ref[1]
    width = refs[0].shape[1]
    for distance in range(blocks):
        block = lax.rem(block_here + blocks - distance, blocks)
        near, far = refs[distance], refs[blocks + distance]
        for source, rows in ((chip, near[...]), (1 - chip, far[0] if distance == 0 else far[...])):
            pair = source * blocks + block
            out_ref[:, pl.ds(pl.multiple_of(pair * width, width), width)] = rows


def attention_kernel(order_ref, place_ref, *refs):
    spans = order_ref.shape[1]
    blocks = spans // 2
    mine_refs, theirs_refs = refs[:blocks], refs[blocks : 2 * blocks]
    near_query, far_query, *packed_queries = refs[2 * blocks : 3 * blocks + 1]
    far_ref, *near_refs = refs[3 * blocks + 1 : -4]
    key_rows, value_rows, query_rows, out_rows = refs[-4:]
    token_rows = query_rows.shape[1]
    span_rows = 2 * token_rows
    place, block_here = place_ref[0], place_ref[1]
    chip, core = place // 2, place % 2
    for distance in range(blocks):
        block = lax.rem(block_here + blocks - distance, blocks)
        packed = packed_queries[distance - 1] if distance else None
        query_rows[2 * block + chip] = packed[0] if distance else near_query[...]
        query_rows[2 * block + 1 - chip] = packed[1] if distance else far_query[0]
        for half in range(2):
            first = order_ref[0, 2 * block + half] * span_rows
            for part in range(2):
                slot = jnp.bitwise_xor(half * 2 + part, place)
                other = jnp.bitwise_xor(slot, 1)
                mine = mine_refs[distance][pl.ds(pl.multiple_of(slot * token_rows, token_rows), token_rows), :]
                theirs = theirs_refs[distance][
                    pl.ds(pl.multiple_of(other * token_rows, token_rows), token_rows), :
                ]
                rows = pl.ds(pl.multiple_of(first + part * token_rows, token_rows), token_rows)
                key_rows[rows, :] = jnp.where(core == 0, mine, theirs)
                value_rows[rows, :] = jnp.where(core == 0, theirs, mine)
    stored = []
    for position in range(spans):
        span = jnp.int32(0)
        for candidate in range(1, spans):
            span = jnp.where(order_ref[0, candidate] == position, candidate, span)
        stored.append(span)
    square = (2 * token_rows, span_rows)
    row_index = lax.broadcasted_iota(jnp.int32, square, 0) % token_rows + core * token_rows
    allowed = lax.broadcasted_iota(jnp.int32, square, 1) <= row_index

    def scores(position):
        pair = query_rows[stored[position]]
        query = jnp.concatenate([pair[:, :HD], pair[:, HD:]], axis=0)
        score = lax.dot_general(
            query,
            key_rows[: (position + 1) * span_rows, :],
            (((1,), (1,)), ((), ())),
            preferred_element_type=jnp.float32,
        )
        start = position * span_rows
        last = jnp.where(allowed, score[:, start:], -jnp.inf)
        return jnp.concatenate([score[:, :start], last], axis=1) if position else last

    score = scores(spans - 1)
    for position in reversed(range(spans)):
        following = scores(position - 1) if position else None
        row_top = jnp.max(score, axis=1, keepdims=True)
        weights = jnp.exp2((score - row_top) * (LOG2_E / math.sqrt(HD)))
        denominator = jnp.sum(weights, axis=1, keepdims=True)
        numerator = jnp.dot(
            weights.astype(jnp.bfloat16),
            value_rows[: (position + 1) * span_rows, :],
            preferred_element_type=jnp.float32,
        )
        rows = (numerator / denominator).astype(jnp.bfloat16)
        out_rows[stored[position]] = jnp.concatenate([rows[:token_rows], rows[token_rows:]], axis=1)
        score = following
    for distance, near_ref in enumerate(near_refs):
        block = lax.rem(block_here + distance, blocks)
        near_ref[...] = out_rows[2 * block + chip]
        far_ref[distance] = out_rows[2 * block + 1 - chip]


VMEM = pl.BlockSpec(memory_space=pltpu.VMEM)
ANY = pl.BlockSpec(memory_space=pl.ANY)
SMEM = pl.BlockSpec(memory_space=pltpu.SMEM)


def whole_cycle_shards(hidden_in, queries, pair_weight, span_order, yarn_divisor):
    own_hidden = hidden_in[0]
    token_rows = own_hidden.shape[0]
    ulysses_size, cycle_size = 2 * lax.axis_size("chip"), lax.axis_size("blk")
    dp_size = lax.axis_size("dp")
    chip, core = lax.axis_index("chip"), lax.axis_index("core")
    ulysses_index, cycle_index = 2 * chip + core, lax.axis_index("blk")
    dp_index = lax.axis_index("dp")
    block_rows = token_rows * ulysses_size
    span_rows = block_rows // 2
    shard_rows = pair_weight.shape[0]
    kv_width = KVH * HD
    columns = cycle_size * HD

    piece = lax.dynamic_slice(
        pair_weight, (0, core * kv_width + chip * columns), (shard_rows, columns)
    )

    slot_devices = jnp.bitwise_xor(ulysses_index, jnp.arange(ulysses_size, dtype=jnp.int32))
    order_row = span_order[0]
    span_values = lax.dynamic_slice(order_row, (2 * cycle_index,), (2,))
    stored = slot_devices[:, None] * token_rows + jnp.arange(token_rows, dtype=jnp.int32)[None, :]
    stored = stored.reshape(block_rows)
    positions = jnp.where(stored < span_rows, span_values[0], span_values[1]) * span_rows + stored % span_rows
    cosine, sine = wide_tables(positions, yarn_divisor)
    own_cosine, own_sine = cosine[:token_rows], sine[:token_rows]
    pair_cosine = jnp.where(core == 0, cosine, 1.0)
    pair_sine = jnp.where(core == 0, sine, 0.0)

    place = jnp.stack([ulysses_index, cycle_index]).astype(jnp.int32)
    one = jax.ShapeDtypeStruct((token_rows, 2 * HD), jnp.bfloat16)
    by_distance = jax.ShapeDtypeStruct((cycle_size, *one.shape), one.dtype)
    far_queries, *near_queries = pl.pallas_call(
        query_rope_kernel,
        out_shape=[by_distance] + [one] * cycle_size,
        in_specs=[SMEM] + [VMEM] * 3,
        out_specs=[VMEM] * (1 + cycle_size),
        compiler_params=pltpu.CompilerParams(vmem_limit_bytes=8 * 1024 * 1024),
        name="query_rope",
    )(place, queries[0], own_cosine, own_sine)

    def ahead(block, distance=1):
        return lax.ppermute(block, "blk", [(i, (i + distance) % cycle_size) for i in range(cycle_size)])

    def along_blocks(parts):
        moved = {distance: ahead(parts[distance], distance) for distance in far_first(cycle_size)}
        return [moved[distance] for distance in range(1, cycle_size)]

    def across(block):
        return lax.ppermute(block, "dp", [(i, dp_size - 1 - i) for i in range(dp_size)])

    def first_row(distance, row):
        return (row * cycle_size + jnp.remainder(cycle_index - distance, cycle_size)) * shard_rows

    other_row = dp_size - 1 - dp_index
    far = exchange(own_hidden, "chip", 1)
    partner = exchange(own_hidden, "core", 1)

    travelling, crossed = piece, across(piece)
    received = [piece]
    firsts = [first_row(0, dp_index)]
    for distance in range(1, cycle_size):
        firsts += [first_row(distance - 1, other_row), first_row(distance, dp_index)]
    rows = jnp.stack([*firsts, first_row(cycle_size - 1, other_row)])
    for distance in range(1, cycle_size - 1):
        travelling = ahead(travelling)
        if distance == 1:
            far_queries, near_queries, pair_cosine, pair_sine, rows, place, travelling = (
                lax.optimization_barrier(
                    (far_queries, near_queries, pair_cosine, pair_sine, rows, place, travelling)
                )
            )
        travelling, crossed = lax.optimization_barrier((travelling, crossed))
        received += [crossed, travelling]
        crossed = across(travelling)

    far, far_queries, travelling = lax.optimization_barrier((far, far_queries, travelling))
    hidden = [own_hidden, partner, far, exchange(far, "core", 1)]
    far_queries = exchange(far_queries, "chip", 1)
    packed = pl.pallas_call(
        pack_kernel,
        out_shape=[jax.ShapeDtypeStruct((2, *one.shape), one.dtype)] * (cycle_size - 1),
        in_specs=[VMEM] * cycle_size,
        out_specs=[VMEM] * (cycle_size - 1),
        compiler_params=pltpu.CompilerParams(vmem_limit_bytes=8 * 1024 * 1024),
        name="pack",
    )(far_queries, *near_queries[1:])

    travelling = ahead(travelling)
    travelling, crossed, packed = lax.optimization_barrier((travelling, crossed, packed))
    received += [crossed, travelling]
    last_piece = across(travelling)
    packed = along_blocks([None, *packed])
    total, last_hidden = pl.pallas_call(
        functools.partial(terms_kernel, ulysses_size, len(received)),
        out_shape=[
            jax.ShapeDtypeStruct((block_rows, columns), jnp.float32),
            jax.ShapeDtypeStruct((block_rows, shard_rows), jnp.bfloat16),
        ],
        in_specs=[SMEM] + [ANY] * (ulysses_size + len(received)),
        out_specs=[VMEM] * 2,
        scratch_shapes=[
            pltpu.VMEM((len(received), block_rows, shard_rows), jnp.bfloat16),
            pltpu.VMEM((len(received), shard_rows, columns), jnp.bfloat16),
            pltpu.SemaphoreType.DMA((len(received), ulysses_size + 1)),
            pltpu.SemaphoreType.DMA((ulysses_size,)),
        ],
        compiler_params=pltpu.CompilerParams(vmem_limit_bytes=20 * 1024 * 1024),
        name="terms",
    )(rows, *hidden, *received)
    last_piece, total, last_hidden = lax.optimization_barrier((last_piece, total, last_hidden))
    pairs = pl.pallas_call(
        pair_rope_kernel,
        out_shape=[jax.ShapeDtypeStruct((block_rows, HD), jnp.bfloat16)] * cycle_size,
        in_specs=[SMEM] + [VMEM] * 5,
        out_specs=[VMEM] * cycle_size,
        scratch_shapes=[pltpu.VMEM((block_rows, columns), jnp.float32)],
        compiler_params=pltpu.CompilerParams(vmem_limit_bytes=12 * 1024 * 1024),
        name="pair_rope",
    )(place, total, last_hidden, last_piece, pair_cosine, pair_sine)
    pairs, packed = lax.optimization_barrier((pairs, packed))
    mine, theirs = {0: pairs[0]}, {0: exchange(pairs[0], "core", 1)}
    for distance in far_first(cycle_size):
        mine[distance] = ahead(pairs[distance], distance)
        theirs[distance] = exchange(mine[distance], "core", 1)
    in_order = range(cycle_size)

    sequence_rows = cycle_size * block_rows
    far, *near = pl.pallas_call(
        attention_kernel,
        out_shape=[by_distance] + [one] * cycle_size,
        in_specs=[SMEM, SMEM] + [VMEM] * (3 * cycle_size + 1),
        out_specs=[VMEM] * (cycle_size + 1),
        scratch_shapes=[
            pltpu.VMEM((sequence_rows, HD), jnp.bfloat16),
            pltpu.VMEM((sequence_rows, HD), jnp.bfloat16),
            pltpu.VMEM((2 * cycle_size, token_rows, 2 * HD), jnp.bfloat16),
            pltpu.VMEM((2 * cycle_size, token_rows, 2 * HD), jnp.bfloat16),
        ],
        compiler_params=pltpu.CompilerParams(vmem_limit_bytes=24 * 1024 * 1024),
        name="attention",
    )(
        span_order,
        place,
        *(mine[d] for d in in_order),
        *(theirs[d] for d in in_order),
        near_queries[0],
        far_queries,
        *packed,
    )
    far = exchange(far, "chip", 1)
    arrived = [near[0], *along_blocks(near)]
    crossed = [far, *along_blocks(far)]
    heads = pl.pallas_call(
        order_heads_kernel,
        out_shape=jax.ShapeDtypeStruct((token_rows, QH * HD), jnp.bfloat16),
        in_specs=[SMEM] + [VMEM] * (2 * cycle_size),
        out_specs=VMEM,
        compiler_params=pltpu.CompilerParams(vmem_limit_bytes=8 * 1024 * 1024),
        name="order_heads",
    )(place, *arrived, *crossed)
    return heads[None]


def solution(mesh):
    sizes = dict(mesh.shape)
    specs = dict(
        in_specs=(
            P("dp", ("blk", "ulysses"), None),
            P("dp", ("blk", "ulysses"), None),
            P(("dp", "blk"), None),
            P("dp", None),
            P(),
        ),
        out_specs=P("dp", ("blk", "ulysses"), None),
        check_vma=False,
    )
    whole_cycle = (
        sizes["blk"] == STEPS + 1
        and sizes["ulysses"] == 4
        and sizes["dp"] == 2
        and sizes["ulysses"] * sizes["blk"] == QH == 2 * KVH
    )
    if not whole_cycle:
        return jax.shard_map(general_shards, mesh=mesh, **specs)
    chips = Mesh(
        mesh.devices.reshape(sizes["dp"], sizes["ulysses"] // 2, 2, sizes["blk"]),
        ("dp", "chip", "core", "blk"),
    )
    rows = P("dp", ("blk", "chip", "core"), None)
    specs["in_specs"] = (rows, rows, *specs["in_specs"][2:])
    specs["out_specs"] = rows
    return jax.shard_map(whole_cycle_shards, mesh=chips, **specs)
```

```python
import functools
import math

import jax
import jax.numpy as jnp
from jax import lax
from jax.experimental import pallas as pl
from jax.experimental.pallas import tpu as pltpu
from jax.sharding import Mesh
from jax.sharding import PartitionSpec as P

KVH = 8
HD = 128
QH = 16
STEPS = 3


LOG_BASE = math.log(500000.0)
LOG2_E = math.log2(math.e)


def from_behind(block, axis, distance):
    devices = range(lax.axis_size(axis))
    route = [((i - distance) % len(devices), i) for i in devices]
    return lax.ppermute(block, axis, route)


def rotate(vectors, angle_table):
    half_dim = vectors.shape[-1] // 2
    first_half = vectors[..., :half_dim]
    second_half = vectors[..., half_dim:]
    cosine = jnp.cos(angle_table)
    sine_part = jnp.sin(angle_table)
    return jnp.concatenate(
        [
            first_half * cosine - second_half * sine_part,
            second_half * cosine + first_half * sine_part,
        ],
        axis=-1,
    )


def angles(positions, yarn_divisor):
    half_dim = yarn_divisor.shape[0]
    scaled = 2.0 * jnp.arange(half_dim, dtype=jnp.float32) / (2 * half_dim)
    inverse = jnp.exp(-LOG_BASE * scaled) / yarn_divisor.astype(jnp.float32)
    return positions.astype(jnp.float32)[:, None] * inverse[None, :]


def positions_of(order_row, first_row, row_count, span_rows):
    stored = first_row + jnp.arange(row_count, dtype=jnp.int32)
    span_index = stored // span_rows
    matches = span_index[:, None] == jnp.arange(order_row.shape[0], dtype=jnp.int32)[None, :]
    span_value = jnp.sum(jnp.where(matches, order_row[None, :], 0), axis=1)
    return span_value * span_rows + stored % span_rows


def tile_scores(query_rows, key_rows):
    product = lax.dot_general(
        query_rows, key_rows, (((1,), (1,)), ((), ())), preferred_element_type=jnp.float32
    )
    return product * (1.0 / math.sqrt(HD))


def row_maximum(query_rows, query_pos, key_rows, key_pos):
    score = tile_scores(query_rows, key_rows)
    return jnp.max(jnp.where(key_pos[None, :] <= query_pos[:, None], score, -jnp.inf), axis=1)


def add_tile(denominator, numerator, query_rows, query_pos, key_rows, value_rows, key_pos, row_top):
    score = tile_scores(query_rows, key_rows)
    allowed = key_pos[None, :] <= query_pos[:, None]
    weights = jnp.where(allowed, jnp.exp(score - row_top[:, None]), 0.0)
    denominator = denominator + jnp.sum(weights, axis=1)
    numerator = numerator + jnp.dot(
        weights.astype(jnp.bfloat16), value_rows, preferred_element_type=jnp.float32
    )
    return (denominator, numerator)


def general_shards(hidden_in, queries, pair_weight, span_order, yarn_divisor):
    inputs_local = hidden_in[0]
    queries_local = queries[0]
    order_row = span_order[0]
    token_rows = inputs_local.shape[0]
    ulysses_size = lax.axis_size("ulysses")
    cycle_size = lax.axis_size("blk")
    ulysses_index = lax.axis_index("ulysses")
    cycle_index = lax.axis_index("blk")
    block_rows = token_rows * ulysses_size
    span_rows = block_rows // 2
    kv_width = KVH * HD
    kv_local = KVH // ulysses_size
    group_size = QH // KVH
    own_positions = positions_of(
        order_row, cycle_index * block_rows + ulysses_index * token_rows, token_rows, span_rows
    )
    own_angles = angles(own_positions, yarn_divisor)
    block_positions = positions_of(order_row, cycle_index * block_rows, block_rows, span_rows)
    rotated_queries = rotate(
        queries_local.astype(jnp.float32).reshape(token_rows, QH, HD), own_angles[:, None, :]
    )
    rotated_queries = rotated_queries.astype(jnp.bfloat16).reshape(token_rows, QH * HD)
    projected = jnp.dot(
        inputs_local,
        lax.all_gather(pair_weight, ("dp", "blk"), axis=0, tiled=True),
        preferred_element_type=jnp.float32,
    )
    token_keys = rotate(
        projected[:, :kv_width].reshape(token_rows, KVH, HD), own_angles[:, None, :]
    )
    token_keys = token_keys.astype(jnp.bfloat16).reshape(token_rows, kv_width)
    token_values = projected[:, kv_width:].astype(jnp.bfloat16)
    query_block, key_block, value_block = (
        lax.all_to_all(rotated_queries, "ulysses", split_axis=1, concat_axis=0, tiled=True),
        lax.all_to_all(token_keys, "ulysses", split_axis=1, concat_axis=0, tiled=True),
        lax.all_to_all(token_values, "ulysses", split_axis=1, concat_axis=0, tiled=True),
    )
    own_pair = jnp.stack([key_block, value_block])
    carried_blocks = [own_pair]
    current_pair = own_pair
    for step_index in range(STEPS):
        current_pair = from_behind(current_pair, "blk", 1)
        carried_blocks.append(current_pair)
    carried_positions = []
    for step_index in range(STEPS + 1):
        source_block = jnp.remainder(cycle_index - step_index, cycle_size)
        carried_positions.append(
            positions_of(order_row, source_block * block_rows, block_rows, span_rows)
        )
    output_rows = []
    for query_half in range(2):
        row_start = query_half * span_rows
        half_positions = block_positions[row_start : row_start + span_rows]
        query_pos = jnp.tile(half_positions, group_size)
        head_outputs = []
        for local_head in range(kv_local):
            query_part = query_block[
                row_start : row_start + span_rows,
                local_head * group_size * HD : (local_head + 1) * group_size * HD,
            ]
            query_rows = (
                query_part.reshape(span_rows, group_size, HD)
                .transpose(1, 0, 2)
                .reshape(group_size * span_rows, HD)
            )
            tile_list = []
            for step_index in range(STEPS + 1):
                pair_block = carried_blocks[step_index]
                for key_half in range(2):
                    key_start = key_half * span_rows
                    key_rows = pair_block[
                        0,
                        key_start : key_start + span_rows,
                        local_head * HD : (local_head + 1) * HD,
                    ]
                    value_rows = pair_block[
                        1,
                        key_start : key_start + span_rows,
                        local_head * HD : (local_head + 1) * HD,
                    ]
                    key_pos = carried_positions[step_index][key_start : key_start + span_rows]
                    tile_list.append((key_rows, value_rows, key_pos))
            row_top = jnp.full((group_size * span_rows,), -jnp.inf, jnp.float32)
            for key_rows, value_rows, key_pos in tile_list:
                tile_top = row_maximum(query_rows, query_pos, key_rows, key_pos)
                row_top = jnp.maximum(row_top, tile_top)
            denominator = jnp.zeros((group_size * span_rows,), jnp.float32)
            numerator = jnp.zeros((group_size * span_rows, HD), jnp.float32)
            for key_rows, value_rows, key_pos in tile_list:
                denominator, numerator = add_tile(
                    denominator,
                    numerator,
                    query_rows,
                    query_pos,
                    key_rows,
                    value_rows,
                    key_pos,
                    row_top,
                )
            normalized = (numerator / denominator[:, None]).astype(jnp.bfloat16)
            normalized = (
                normalized.reshape(group_size, span_rows, HD)
                .transpose(1, 0, 2)
                .reshape(span_rows, group_size * HD)
            )
            head_outputs.append(normalized)
        output_rows.append(jnp.concatenate(head_outputs, axis=1))
    block_output = jnp.concatenate(output_rows, axis=0)
    token_output = lax.all_to_all(block_output, "ulysses", split_axis=0, concat_axis=1, tiled=True)
    return token_output[None]


def far_first(size):
    return sorted(range(1, size), key=lambda distance: -min(distance, size - distance))


def exchange(block, axis, distance):
    size = lax.axis_size(axis)
    return lax.ppermute(block, axis, [(i, i ^ distance) for i in range(size)])


def wide_tables(positions, yarn_divisor):
    angle_table = angles(positions, yarn_divisor)
    cosine, sine = jnp.cos(angle_table), jnp.sin(angle_table)
    return jnp.concatenate([cosine, cosine], axis=1), jnp.concatenate([-sine, sine], axis=1)


def rope_head(head, cosine, signed_sine):
    return head * cosine + pltpu.roll(head, HD // 2, 1) * signed_sine


def query_rope_kernel(place_ref, query_ref, cosine_ref, sine_ref, far_ref, *near_refs):
    cosine, sine = cosine_ref[...], sine_ref[...]
    blocks, width = far_ref.shape[0], far_ref.shape[2]
    chip, block_here = place_ref[0] // 2, place_ref[1]
    for distance, near_ref in enumerate(near_refs):
        block = lax.rem(block_here + distance, blocks)
        for target, out_ref in ((chip, near_ref), (1 - chip, far_ref.at[distance])):
            columns = pl.ds(pl.multiple_of((target * blocks + block) * width, width), width)
            pair = query_ref[:, columns].astype(jnp.float32)
            for start in range(0, width, HD):
                rows = rope_head(pair[:, start : start + HD], cosine, sine)
                out_ref[:, start : start + HD] = rows.astype(jnp.bfloat16)


def pack_kernel(far_ref, *refs):
    near_refs, out_refs = refs[: len(refs) // 2], refs[len(refs) // 2 :]
    for distance, (near_ref, out_ref) in enumerate(zip(near_refs, out_refs), 1):
        out_ref[0] = near_ref[...]
        out_ref[1] = far_ref[distance]


def load_terms(rows_ref, slot_refs, piece_refs, hidden_rows, pieces, sems):
    token_rows = slot_refs[0].shape[0]
    copies = []
    for index, piece_ref in enumerate(piece_refs):
        depth = piece_ref.shape[0]
        columns = pl.ds(pl.multiple_of(rows_ref[index], depth), depth)
        started = [pltpu.make_async_copy(piece_ref, pieces.at[index], sems.at[index, 0])]
        for slot, slot_ref in enumerate(slot_refs):
            rows = hidden_rows.at[index, pl.ds(slot * token_rows, token_rows)]
            started.append(pltpu.make_async_copy(slot_ref.at[:, columns], rows, sems.at[index, slot + 1]))
        for copy in started:
            copy.start()
        copies.append(started)
    return copies


def terms_kernel(slots, count, rows_ref, *refs):
    slot_refs, piece_refs = refs[:slots], refs[slots : slots + count]
    out_ref, next_hidden_ref, hidden_rows, pieces, sems, next_sems = refs[slots + count :]
    copies = load_terms(rows_ref, slot_refs, piece_refs, hidden_rows, pieces, sems)
    token_rows, depth = slot_refs[0].shape[0], piece_refs[0].shape[0]
    columns = pl.ds(pl.multiple_of(rows_ref[count], depth), depth)
    next_copies = [
        pltpu.make_async_copy(
            slot_ref.at[:, columns],
            next_hidden_ref.at[pl.ds(slot * token_rows, token_rows)],
            next_sems.at[slot],
        )
        for slot, slot_ref in enumerate(slot_refs)
    ]
    for copy in next_copies:
        copy.start()
    total = None
    for index, started in enumerate(copies):
        for copy in started:
            copy.wait()
        term = jnp.dot(hidden_rows[index], pieces[index], preferred_element_type=jnp.float32)
        total = term if total is None else total + term
    out_ref[...] = total
    for copy in next_copies:
        copy.wait()


def pair_rope_kernel(place_ref, total_ref, hidden_ref, piece_ref, cosine_ref, sine_ref, *refs):
    out_refs, sum_ref = refs[:-1], refs[-1]
    sum_ref[...] = total_ref[...] + jnp.dot(
        hidden_ref[...], piece_ref[...], preferred_element_type=jnp.float32
    )
    cosine, sine = cosine_ref[...], sine_ref[...]
    for distance, out_ref in enumerate(out_refs):
        head = lax.rem(place_ref[1] + distance, len(out_refs))
        rows = sum_ref[:, pl.ds(pl.multiple_of(head * HD, HD), HD)]
        out_ref[...] = rope_head(rows, cosine, sine).astype(jnp.bfloat16)


def order_heads_kernel(place_ref, *refs):
    out_ref = refs[-1]
    blocks = (len(refs) - 1) // 2
    chip, block_here = place_ref[0] // 2, place_ref[1]
    width = refs[0].shape[1]
    for distance in range(blocks):
        block = lax.rem(block_here + blocks - distance, blocks)
        near, far = refs[distance], refs[blocks + distance]
        for source, rows in ((chip, near[...]), (1 - chip, far[...] if distance else far[far.shape[0] - 1])):
            pair = source * blocks + block
            out_ref[:, pl.ds(pl.multiple_of(pair * width, width), width)] = rows


def attention_kernel(order_ref, place_ref, *refs):
    spans = order_ref.shape[1]
    blocks = spans // 2
    mine_refs, theirs_refs = refs[:blocks], refs[blocks : 2 * blocks]
    near_query, far_query, *packed_queries = refs[2 * blocks : 3 * blocks + 1]
    first_far_ref, last_far_ref, *near_refs = refs[3 * blocks + 1 : -4]
    key_rows, value_rows, query_rows, out_rows = refs[-4:]
    token_rows = query_rows.shape[1]
    span_rows = 2 * token_rows
    place, block_here = place_ref[0], place_ref[1]
    chip, core = place // 2, place % 2
    for distance in range(blocks):
        block = lax.rem(block_here + blocks - distance, blocks)
        packed = packed_queries[distance - 1] if distance else None
        query_rows[2 * block + chip] = packed[0] if distance else near_query[...]
        query_rows[2 * block + 1 - chip] = packed[1] if distance else far_query[0]
        for half in range(2):
            first = order_ref[0, 2 * block + half] * span_rows
            for part in range(2):
                slot = jnp.bitwise_xor(half * 2 + part, place)
                other = jnp.bitwise_xor(slot, 1)
                mine = mine_refs[distance][pl.ds(pl.multiple_of(slot * token_rows, token_rows), token_rows), :]
                theirs = theirs_refs[distance][
                    pl.ds(pl.multiple_of(other * token_rows, token_rows), token_rows), :
                ]
                rows = pl.ds(pl.multiple_of(first + part * token_rows, token_rows), token_rows)
                key_rows[rows, :] = jnp.where(core == 0, mine, theirs)
                value_rows[rows, :] = jnp.where(core == 0, theirs, mine)
    stored = []
    for position in range(spans):
        span = jnp.int32(0)
        for candidate in range(1, spans):
            span = jnp.where(order_ref[0, candidate] == position, candidate, span)
        stored.append(span)
    square = (2 * token_rows, span_rows)
    row_index = lax.broadcasted_iota(jnp.int32, square, 0) % token_rows + core * token_rows
    allowed = lax.broadcasted_iota(jnp.int32, square, 1) <= row_index

    def scores(position):
        pair = query_rows[stored[position]]
        query = jnp.concatenate([pair[:, :HD], pair[:, HD:]], axis=0)
        score = lax.dot_general(
            query,
            key_rows[: (position + 1) * span_rows, :],
            (((1,), (1,)), ((), ())),
            preferred_element_type=jnp.float32,
        )
        start = position * span_rows
        last = jnp.where(allowed, score[:, start:], -jnp.inf)
        return jnp.concatenate([score[:, :start], last], axis=1) if position else last

    score = scores(spans - 1)
    for position in reversed(range(spans)):
        following = scores(position - 1) if position else None
        row_top = jnp.max(score, axis=1, keepdims=True)
        weights = jnp.exp2((score - row_top) * (LOG2_E / math.sqrt(HD)))
        denominator = jnp.sum(weights, axis=1, keepdims=True)
        numerator = jnp.dot(
            weights.astype(jnp.bfloat16),
            value_rows[: (position + 1) * span_rows, :],
            preferred_element_type=jnp.float32,
        )
        rows = (numerator / denominator).astype(jnp.bfloat16)
        out_rows[stored[position]] = jnp.concatenate([rows[:token_rows], rows[token_rows:]], axis=1)
        score = following
    for distance, near_ref in enumerate(near_refs):
        block = lax.rem(block_here + distance, blocks)
        near_ref[...] = out_rows[2 * block + chip]
    order = [*far_first(blocks), 0]
    for index, distance in enumerate(order):
        block = lax.rem(block_here + distance, blocks)
        half, place_in_half = divmod(index, blocks // 2)
        (first_far_ref, last_far_ref)[half][place_in_half] = out_rows[2 * block + 1 - chip]


VMEM = pl.BlockSpec(memory_space=pltpu.VMEM)
ANY = pl.BlockSpec(memory_space=pl.ANY)
SMEM = pl.BlockSpec(memory_space=pltpu.SMEM)


def whole_cycle_shards(hidden_in, queries, pair_weight, span_order, yarn_divisor):
    own_hidden = hidden_in[0]
    token_rows = own_hidden.shape[0]
    ulysses_size, cycle_size = 2 * lax.axis_size("chip"), lax.axis_size("blk")
    dp_size = lax.axis_size("dp")
    chip, core = lax.axis_index("chip"), lax.axis_index("core")
    ulysses_index, cycle_index = 2 * chip + core, lax.axis_index("blk")
    dp_index = lax.axis_index("dp")
    block_rows = token_rows * ulysses_size
    span_rows = block_rows // 2
    shard_rows = pair_weight.shape[0]
    kv_width = KVH * HD
    columns = cycle_size * HD

    piece = lax.dynamic_slice(
        pair_weight, (0, core * kv_width + chip * columns), (shard_rows, columns)
    )

    slot_devices = jnp.bitwise_xor(ulysses_index, jnp.arange(ulysses_size, dtype=jnp.int32))
    order_row = span_order[0]
    span_values = lax.dynamic_slice(order_row, (2 * cycle_index,), (2,))
    stored = slot_devices[:, None] * token_rows + jnp.arange(token_rows, dtype=jnp.int32)[None, :]
    stored = stored.reshape(block_rows)
    positions = jnp.where(stored < span_rows, span_values[0], span_values[1]) * span_rows + stored % span_rows
    cosine, sine = wide_tables(positions, yarn_divisor)
    own_cosine, own_sine = cosine[:token_rows], sine[:token_rows]
    pair_cosine = jnp.where(core == 0, cosine, 1.0)
    pair_sine = jnp.where(core == 0, sine, 0.0)

    place = jnp.stack([ulysses_index, cycle_index]).astype(jnp.int32)
    one = jax.ShapeDtypeStruct((token_rows, 2 * HD), jnp.bfloat16)
    by_distance = jax.ShapeDtypeStruct((cycle_size, *one.shape), one.dtype)
    far_queries, *near_queries = pl.pallas_call(
        query_rope_kernel,
        out_shape=[by_distance] + [one] * cycle_size,
        in_specs=[SMEM] + [VMEM] * 3,
        out_specs=[VMEM] * (1 + cycle_size),
        compiler_params=pltpu.CompilerParams(vmem_limit_bytes=8 * 1024 * 1024),
        name="query_rope",
    )(place, queries[0], own_cosine, own_sine)

    def ahead(block, distance=1):
        return lax.ppermute(block, "blk", [(i, (i + distance) % cycle_size) for i in range(cycle_size)])

    def along_blocks(parts):
        moved = {distance: ahead(parts[distance], distance) for distance in far_first(cycle_size)}
        return [moved[distance] for distance in range(1, cycle_size)]

    def across(block):
        return lax.ppermute(block, "dp", [(i, dp_size - 1 - i) for i in range(dp_size)])

    def first_row(distance, row):
        return (row * cycle_size + jnp.remainder(cycle_index - distance, cycle_size)) * shard_rows

    other_row = dp_size - 1 - dp_index
    far = exchange(own_hidden, "chip", 1)
    partner = exchange(own_hidden, "core", 1)

    travelling, crossed = piece, across(piece)
    received = [piece]
    firsts = [first_row(0, dp_index)]
    for distance in range(1, cycle_size):
        firsts += [first_row(distance - 1, other_row), first_row(distance, dp_index)]
    rows = jnp.stack([*firsts, first_row(cycle_size - 1, other_row)])
    for distance in range(1, cycle_size - 1):
        travelling = ahead(travelling)
        if distance == 1:
            far_queries, near_queries, pair_cosine, pair_sine, rows, place, travelling = (
                lax.optimization_barrier(
                    (far_queries, near_queries, pair_cosine, pair_sine, rows, place, travelling)
                )
            )
        travelling, crossed = lax.optimization_barrier((travelling, crossed))
        received += [crossed, travelling]
        crossed = across(travelling)

    far, far_queries, travelling = lax.optimization_barrier((far, far_queries, travelling))
    hidden = [own_hidden, partner, far, exchange(far, "core", 1)]
    far_queries = exchange(far_queries, "chip", 1)
    packed = pl.pallas_call(
        pack_kernel,
        out_shape=[jax.ShapeDtypeStruct((2, *one.shape), one.dtype)] * (cycle_size - 1),
        in_specs=[VMEM] * cycle_size,
        out_specs=[VMEM] * (cycle_size - 1),
        compiler_params=pltpu.CompilerParams(vmem_limit_bytes=8 * 1024 * 1024),
        name="pack",
    )(far_queries, *near_queries[1:])

    travelling = ahead(travelling)
    travelling, crossed, packed = lax.optimization_barrier((travelling, crossed, packed))
    received += [crossed, travelling]
    last_piece = across(travelling)
    packed = along_blocks([None, *packed])
    total, last_hidden = pl.pallas_call(
        functools.partial(terms_kernel, ulysses_size, len(received)),
        out_shape=[
            jax.ShapeDtypeStruct((block_rows, columns), jnp.float32),
            jax.ShapeDtypeStruct((block_rows, shard_rows), jnp.bfloat16),
        ],
        in_specs=[SMEM] + [ANY] * (ulysses_size + len(received)),
        out_specs=[VMEM] * 2,
        scratch_shapes=[
            pltpu.VMEM((len(received), block_rows, shard_rows), jnp.bfloat16),
            pltpu.VMEM((len(received), shard_rows, columns), jnp.bfloat16),
            pltpu.SemaphoreType.DMA((len(received), ulysses_size + 1)),
            pltpu.SemaphoreType.DMA((ulysses_size,)),
        ],
        compiler_params=pltpu.CompilerParams(vmem_limit_bytes=20 * 1024 * 1024),
        name="terms",
    )(rows, *hidden, *received)
    last_piece, total, last_hidden = lax.optimization_barrier((last_piece, total, last_hidden))
    pairs = pl.pallas_call(
        pair_rope_kernel,
        out_shape=[jax.ShapeDtypeStruct((block_rows, HD), jnp.bfloat16)] * cycle_size,
        in_specs=[SMEM] + [VMEM] * 5,
        out_specs=[VMEM] * cycle_size,
        scratch_shapes=[pltpu.VMEM((block_rows, columns), jnp.float32)],
        compiler_params=pltpu.CompilerParams(vmem_limit_bytes=12 * 1024 * 1024),
        name="pair_rope",
    )(place, total, last_hidden, last_piece, pair_cosine, pair_sine)
    pairs, packed = lax.optimization_barrier((pairs, packed))
    mine, theirs = {0: pairs[0]}, {0: exchange(pairs[0], "core", 1)}
    for distance in far_first(cycle_size):
        mine[distance] = ahead(pairs[distance], distance)
        theirs[distance] = exchange(mine[distance], "core", 1)
    in_order = range(cycle_size)

    sequence_rows = cycle_size * block_rows
    half = jax.ShapeDtypeStruct((cycle_size // 2, *one.shape), one.dtype)
    first_far, last_far, *near = pl.pallas_call(
        attention_kernel,
        out_shape=[half, half] + [one] * cycle_size,
        in_specs=[SMEM, SMEM] + [VMEM] * (3 * cycle_size + 1),
        out_specs=[VMEM] * (cycle_size + 2),
        scratch_shapes=[
            pltpu.VMEM((sequence_rows, HD), jnp.bfloat16),
            pltpu.VMEM((sequence_rows, HD), jnp.bfloat16),
            pltpu.VMEM((2 * cycle_size, token_rows, 2 * HD), jnp.bfloat16),
            pltpu.VMEM((2 * cycle_size, token_rows, 2 * HD), jnp.bfloat16),
        ],
        compiler_params=pltpu.CompilerParams(vmem_limit_bytes=24 * 1024 * 1024),
        name="attention",
    )(
        span_order,
        place,
        *(mine[d] for d in in_order),
        *(theirs[d] for d in in_order),
        near_queries[0],
        far_queries,
        *packed,
    )
    halves = [exchange(half, "chip", 1) for half in (first_far, last_far)]
    arrived = [near[0], *along_blocks(near)]
    crossed = {0: halves[1]}
    for index, distance in enumerate(far_first(cycle_size)):
        part, place_in_half = divmod(index, cycle_size // 2)
        crossed[distance] = ahead(halves[part][place_in_half], distance)
    heads = pl.pallas_call(
        order_heads_kernel,
        out_shape=jax.ShapeDtypeStruct((token_rows, QH * HD), jnp.bfloat16),
        in_specs=[SMEM] + [VMEM] * (2 * cycle_size),
        out_specs=VMEM,
        compiler_params=pltpu.CompilerParams(vmem_limit_bytes=8 * 1024 * 1024),
        name="order_heads",
    )(place, *arrived, *(crossed[distance] for distance in in_order))
    return heads[None]


def solution(mesh):
    sizes = dict(mesh.shape)
    specs = dict(
        in_specs=(
            P("dp", ("blk", "ulysses"), None),
            P("dp", ("blk", "ulysses"), None),
            P(("dp", "blk"), None),
            P("dp", None),
            P(),
        ),
        out_specs=P("dp", ("blk", "ulysses"), None),
        check_vma=False,
    )
    whole_cycle = (
        sizes["blk"] == STEPS + 1
        and sizes["ulysses"] == 4
        and sizes["dp"] == 2
        and sizes["ulysses"] * sizes["blk"] == QH == 2 * KVH
    )
    if not whole_cycle:
        return jax.shard_map(general_shards, mesh=mesh, **specs)
    chips = Mesh(
        mesh.devices.reshape(sizes["dp"], sizes["ulysses"] // 2, 2, sizes["blk"]),
        ("dp", "chip", "core", "blk"),
    )
    rows = P("dp", ("blk", "chip", "core"), None)
    specs["in_specs"] = (rows, rows, *specs["in_specs"][2:])
    specs["out_specs"] = rows
    return jax.shard_map(whole_cycle_shards, mesh=chips, **specs)
```

```python
import functools
import math

import jax
import jax.numpy as jnp
from jax import lax
from jax.experimental import pallas as pl
from jax.experimental.pallas import tpu as pltpu
from jax.sharding import Mesh
from jax.sharding import PartitionSpec as P

KVH = 8
HD = 128
QH = 16
STEPS = 3


LOG_BASE = math.log(500000.0)
LOG2_E = math.log2(math.e)


def from_behind(block, axis, distance):
    devices = range(lax.axis_size(axis))
    route = [((i - distance) % len(devices), i) for i in devices]
    return lax.ppermute(block, axis, route)


def rotate(vectors, angle_table):
    half_dim = vectors.shape[-1] // 2
    first_half = vectors[..., :half_dim]
    second_half = vectors[..., half_dim:]
    cosine = jnp.cos(angle_table)
    sine_part = jnp.sin(angle_table)
    return jnp.concatenate(
        [
            first_half * cosine - second_half * sine_part,
            second_half * cosine + first_half * sine_part,
        ],
        axis=-1,
    )


def angles(positions, yarn_divisor):
    half_dim = yarn_divisor.shape[0]
    scaled = 2.0 * jnp.arange(half_dim, dtype=jnp.float32) / (2 * half_dim)
    inverse = jnp.exp(-LOG_BASE * scaled) / yarn_divisor.astype(jnp.float32)
    return positions.astype(jnp.float32)[:, None] * inverse[None, :]


def positions_of(order_row, first_row, row_count, span_rows):
    stored = first_row + jnp.arange(row_count, dtype=jnp.int32)
    span_index = stored // span_rows
    matches = span_index[:, None] == jnp.arange(order_row.shape[0], dtype=jnp.int32)[None, :]
    span_value = jnp.sum(jnp.where(matches, order_row[None, :], 0), axis=1)
    return span_value * span_rows + stored % span_rows


def tile_scores(query_rows, key_rows):
    product = lax.dot_general(
        query_rows, key_rows, (((1,), (1,)), ((), ())), preferred_element_type=jnp.float32
    )
    return product * (1.0 / math.sqrt(HD))


def row_maximum(query_rows, query_pos, key_rows, key_pos):
    score = tile_scores(query_rows, key_rows)
    return jnp.max(jnp.where(key_pos[None, :] <= query_pos[:, None], score, -jnp.inf), axis=1)


def add_tile(denominator, numerator, query_rows, query_pos, key_rows, value_rows, key_pos, row_top):
    score = tile_scores(query_rows, key_rows)
    allowed = key_pos[None, :] <= query_pos[:, None]
    weights = jnp.where(allowed, jnp.exp(score - row_top[:, None]), 0.0)
    denominator = denominator + jnp.sum(weights, axis=1)
    numerator = numerator + jnp.dot(
        weights.astype(jnp.bfloat16), value_rows, preferred_element_type=jnp.float32
    )
    return (denominator, numerator)


def general_shards(hidden_in, queries, pair_weight, span_order, yarn_divisor):
    inputs_local = hidden_in[0]
    queries_local = queries[0]
    order_row = span_order[0]
    token_rows = inputs_local.shape[0]
    ulysses_size = lax.axis_size("ulysses")
    cycle_size = lax.axis_size("blk")
    ulysses_index = lax.axis_index("ulysses")
    cycle_index = lax.axis_index("blk")
    block_rows = token_rows * ulysses_size
    span_rows = block_rows // 2
    kv_width = KVH * HD
    kv_local = KVH // ulysses_size
    group_size = QH // KVH
    own_positions = positions_of(
        order_row, cycle_index * block_rows + ulysses_index * token_rows, token_rows, span_rows
    )
    own_angles = angles(own_positions, yarn_divisor)
    block_positions = positions_of(order_row, cycle_index * block_rows, block_rows, span_rows)
    rotated_queries = rotate(
        queries_local.astype(jnp.float32).reshape(token_rows, QH, HD), own_angles[:, None, :]
    )
    rotated_queries = rotated_queries.astype(jnp.bfloat16).reshape(token_rows, QH * HD)
    projected = jnp.dot(
        inputs_local,
        lax.all_gather(pair_weight, ("dp", "blk"), axis=0, tiled=True),
        preferred_element_type=jnp.float32,
    )
    token_keys = rotate(
        projected[:, :kv_width].reshape(token_rows, KVH, HD), own_angles[:, None, :]
    )
    token_keys = token_keys.astype(jnp.bfloat16).reshape(token_rows, kv_width)
    token_values = projected[:, kv_width:].astype(jnp.bfloat16)
    query_block, key_block, value_block = (
        lax.all_to_all(rotated_queries, "ulysses", split_axis=1, concat_axis=0, tiled=True),
        lax.all_to_all(token_keys, "ulysses", split_axis=1, concat_axis=0, tiled=True),
        lax.all_to_all(token_values, "ulysses", split_axis=1, concat_axis=0, tiled=True),
    )
    own_pair = jnp.stack([key_block, value_block])
    carried_blocks = [own_pair]
    current_pair = own_pair
    for step_index in range(STEPS):
        current_pair = from_behind(current_pair, "blk", 1)
        carried_blocks.append(current_pair)
    carried_positions = []
    for step_index in range(STEPS + 1):
        source_block = jnp.remainder(cycle_index - step_index, cycle_size)
        carried_positions.append(
            positions_of(order_row, source_block * block_rows, block_rows, span_rows)
        )
    output_rows = []
    for query_half in range(2):
        row_start = query_half * span_rows
        half_positions = block_positions[row_start : row_start + span_rows]
        query_pos = jnp.tile(half_positions, group_size)
        head_outputs = []
        for local_head in range(kv_local):
            query_part = query_block[
                row_start : row_start + span_rows,
                local_head * group_size * HD : (local_head + 1) * group_size * HD,
            ]
            query_rows = (
                query_part.reshape(span_rows, group_size, HD)
                .transpose(1, 0, 2)
                .reshape(group_size * span_rows, HD)
            )
            tile_list = []
            for step_index in range(STEPS + 1):
                pair_block = carried_blocks[step_index]
                for key_half in range(2):
                    key_start = key_half * span_rows
                    key_rows = pair_block[
                        0,
                        key_start : key_start + span_rows,
                        local_head * HD : (local_head + 1) * HD,
                    ]
                    value_rows = pair_block[
                        1,
                        key_start : key_start + span_rows,
                        local_head * HD : (local_head + 1) * HD,
                    ]
                    key_pos = carried_positions[step_index][key_start : key_start + span_rows]
                    tile_list.append((key_rows, value_rows, key_pos))
            row_top = jnp.full((group_size * span_rows,), -jnp.inf, jnp.float32)
            for key_rows, value_rows, key_pos in tile_list:
                tile_top = row_maximum(query_rows, query_pos, key_rows, key_pos)
                row_top = jnp.maximum(row_top, tile_top)
            denominator = jnp.zeros((group_size * span_rows,), jnp.float32)
            numerator = jnp.zeros((group_size * span_rows, HD), jnp.float32)
            for key_rows, value_rows, key_pos in tile_list:
                denominator, numerator = add_tile(
                    denominator,
                    numerator,
                    query_rows,
                    query_pos,
                    key_rows,
                    value_rows,
                    key_pos,
                    row_top,
                )
            normalized = (numerator / denominator[:, None]).astype(jnp.bfloat16)
            normalized = (
                normalized.reshape(group_size, span_rows, HD)
                .transpose(1, 0, 2)
                .reshape(span_rows, group_size * HD)
            )
            head_outputs.append(normalized)
        output_rows.append(jnp.concatenate(head_outputs, axis=1))
    block_output = jnp.concatenate(output_rows, axis=0)
    token_output = lax.all_to_all(block_output, "ulysses", split_axis=0, concat_axis=1, tiled=True)
    return token_output[None]


def far_first(size):
    return sorted(range(1, size), key=lambda distance: -min(distance, size - distance))


def exchange(block, axis, distance):
    size = lax.axis_size(axis)
    return lax.ppermute(block, axis, [(i, i ^ distance) for i in range(size)])


def wide_tables(positions, yarn_divisor):
    angle_table = angles(positions, yarn_divisor)
    cosine, sine = jnp.cos(angle_table), jnp.sin(angle_table)
    return jnp.concatenate([cosine, cosine], axis=1), jnp.concatenate([-sine, sine], axis=1)


def rope_head(head, cosine, signed_sine):
    return head * cosine + pltpu.roll(head, HD // 2, 1) * signed_sine


def query_rope_kernel(place_ref, query_ref, cosine_ref, sine_ref, far_ref, *near_refs):
    cosine, sine = cosine_ref[...], sine_ref[...]
    blocks, width = far_ref.shape[0], far_ref.shape[2]
    chip, block_here = place_ref[0] // 2, place_ref[1]
    for distance, near_ref in enumerate(near_refs):
        block = lax.rem(block_here + distance, blocks)
        for target, out_ref in ((chip, near_ref), (1 - chip, far_ref.at[distance])):
            columns = pl.ds(pl.multiple_of((target * blocks + block) * width, width), width)
            pair = query_ref[:, columns].astype(jnp.float32)
            for start in range(0, width, HD):
                rows = rope_head(pair[:, start : start + HD], cosine, sine)
                out_ref[:, start : start + HD] = rows.astype(jnp.bfloat16)


def pack_kernel(far_ref, *refs):
    near_refs, out_refs = refs[: len(refs) // 2], refs[len(refs) // 2 :]
    for distance, (near_ref, out_ref) in enumerate(zip(near_refs, out_refs), 1):
        out_ref[0] = near_ref[...]
        out_ref[1] = far_ref[distance]


def load_terms(rows_ref, slot_refs, piece_refs, hidden_rows, pieces, sems):
    token_rows = slot_refs[0].shape[0]
    copies = []
    for index, piece_ref in enumerate(piece_refs):
        depth = piece_ref.shape[0]
        columns = pl.ds(pl.multiple_of(rows_ref[index], depth), depth)
        started = [pltpu.make_async_copy(piece_ref, pieces.at[index], sems.at[index, 0])]
        for slot, slot_ref in enumerate(slot_refs):
            rows = hidden_rows.at[index, pl.ds(slot * token_rows, token_rows)]
            started.append(pltpu.make_async_copy(slot_ref.at[:, columns], rows, sems.at[index, slot + 1]))
        for copy in started:
            copy.start()
        copies.append(started)
    return copies


def terms_kernel(slots, count, rows_ref, *refs):
    slot_refs, piece_refs = refs[:slots], refs[slots : slots + count]
    out_ref, next_hidden_ref, hidden_rows, pieces, sems, next_sems = refs[slots + count :]
    copies = load_terms(rows_ref, slot_refs, piece_refs, hidden_rows, pieces, sems)
    token_rows, depth = slot_refs[0].shape[0], piece_refs[0].shape[0]
    columns = pl.ds(pl.multiple_of(rows_ref[count], depth), depth)
    next_copies = [
        pltpu.make_async_copy(
            slot_ref.at[:, columns],
            next_hidden_ref.at[pl.ds(slot * token_rows, token_rows)],
            next_sems.at[slot],
        )
        for slot, slot_ref in enumerate(slot_refs)
    ]
    for copy in next_copies:
        copy.start()
    total = None
    for index, started in enumerate(copies):
        for copy in started:
            copy.wait()
        term = jnp.dot(hidden_rows[index], pieces[index], preferred_element_type=jnp.float32)
        total = term if total is None else total + term
    out_ref[...] = total
    for copy in next_copies:
        copy.wait()


def pair_rope_kernel(place_ref, total_ref, hidden_ref, piece_ref, cosine_ref, sine_ref, *refs):
    out_refs, sum_ref = refs[:-1], refs[-1]
    sum_ref[...] = total_ref[...] + jnp.dot(
        hidden_ref[...], piece_ref[...], preferred_element_type=jnp.float32
    )
    cosine, sine = cosine_ref[...], sine_ref[...]
    for distance, out_ref in enumerate(out_refs):
        head = lax.rem(place_ref[1] + distance, len(out_refs))
        rows = sum_ref[:, pl.ds(pl.multiple_of(head * HD, HD), HD)]
        out_ref[...] = rope_head(rows, cosine, sine).astype(jnp.bfloat16)


def order_heads_kernel(place_ref, *refs):
    out_ref = refs[-1]
    blocks = (len(refs) - 1) // 2
    chip, block_here = place_ref[0] // 2, place_ref[1]
    width = refs[0].shape[1]
    for distance in range(blocks):
        block = lax.rem(block_here + blocks - distance, blocks)
        near, far = refs[distance], refs[blocks + distance]
        for source, rows in ((chip, near[...]), (1 - chip, far[...] if distance else far[far.shape[0] - 1])):
            pair = source * blocks + block
            out_ref[:, pl.ds(pl.multiple_of(pair * width, width), width)] = rows


def sort_queries_kernel(order_ref, place_ref, near_ref, far_ref, *refs):
    packed_refs, out_ref = refs[:-1], refs[-1]
    blocks = len(packed_refs) + 1
    token_rows = near_ref.shape[0]
    chip, block_here = place_ref[0] // 2, place_ref[1]
    for distance in range(blocks):
        block = lax.rem(block_here + blocks - distance, blocks)
        near = packed_refs[distance - 1][0] if distance else near_ref[...]
        far = packed_refs[distance - 1][1] if distance else far_ref[0]
        for source, pair in ((chip, near), (1 - chip, far)):
            position = order_ref[0, 2 * block + source]
            out_ref[position, :token_rows] = pair[:, :HD]
            out_ref[position, token_rows:] = pair[:, HD:]


def attention_kernel(order_ref, place_ref, query_ref, *refs):
    spans = order_ref.shape[1]
    blocks = spans // 2
    mine_refs, theirs_refs = refs[:blocks], refs[blocks : 2 * blocks]
    first_far_ref, last_far_ref, *near_refs = refs[2 * blocks : -3]
    key_rows, value_rows, out_rows = refs[-3:]
    token_rows = query_ref.shape[1] // 2
    span_rows = 2 * token_rows
    place, block_here = place_ref[0], place_ref[1]
    chip, core = place // 2, place % 2
    for distance in range(blocks):
        block = lax.rem(block_here + blocks - distance, blocks)
        for half in range(2):
            first = order_ref[0, 2 * block + half] * span_rows
            for part in range(2):
                slot = jnp.bitwise_xor(half * 2 + part, place)
                other = jnp.bitwise_xor(slot, 1)
                mine = mine_refs[distance][pl.ds(pl.multiple_of(slot * token_rows, token_rows), token_rows), :]
                theirs = theirs_refs[distance][
                    pl.ds(pl.multiple_of(other * token_rows, token_rows), token_rows), :
                ]
                rows = pl.ds(pl.multiple_of(first + part * token_rows, token_rows), token_rows)
                key_rows[rows, :] = jnp.where(core == 0, mine, theirs)
                value_rows[rows, :] = jnp.where(core == 0, theirs, mine)
    stored = []
    for position in range(spans):
        span = jnp.int32(0)
        for candidate in range(1, spans):
            span = jnp.where(order_ref[0, candidate] == position, candidate, span)
        stored.append(span)
    square = (2 * token_rows, span_rows)
    row_index = lax.broadcasted_iota(jnp.int32, square, 0) % token_rows + core * token_rows
    allowed = lax.broadcasted_iota(jnp.int32, square, 1) <= row_index

    def scores(position):
        score = lax.dot_general(
            query_ref[position],
            key_rows[: (position + 1) * span_rows, :],
            (((1,), (1,)), ((), ())),
            preferred_element_type=jnp.float32,
        )
        start = position * span_rows
        last = jnp.where(allowed, score[:, start:], -jnp.inf)
        return jnp.concatenate([score[:, :start], last], axis=1) if position else last

    score = scores(spans - 1)
    for position in reversed(range(spans)):
        following = scores(position - 1) if position else None
        row_top = jnp.max(score, axis=1, keepdims=True)
        weights = jnp.exp2((score - row_top) * (LOG2_E / math.sqrt(HD)))
        denominator = jnp.sum(weights, axis=1, keepdims=True)
        numerator = jnp.dot(
            weights.astype(jnp.bfloat16),
            value_rows[: (position + 1) * span_rows, :],
            preferred_element_type=jnp.float32,
        )
        rows = (numerator / denominator).astype(jnp.bfloat16)
        out_rows[stored[position]] = jnp.concatenate([rows[:token_rows], rows[token_rows:]], axis=1)
        score = following
    for distance, near_ref in enumerate(near_refs):
        block = lax.rem(block_here + distance, blocks)
        near_ref[...] = out_rows[2 * block + chip]
    order = [*far_first(blocks), 0]
    for index, distance in enumerate(order):
        block = lax.rem(block_here + distance, blocks)
        half, place_in_half = divmod(index, blocks // 2)
        (first_far_ref, last_far_ref)[half][place_in_half] = out_rows[2 * block + 1 - chip]


VMEM = pl.BlockSpec(memory_space=pltpu.VMEM)
ANY = pl.BlockSpec(memory_space=pl.ANY)
SMEM = pl.BlockSpec(memory_space=pltpu.SMEM)


def whole_cycle_shards(hidden_in, queries, pair_weight, span_order, yarn_divisor):
    own_hidden = hidden_in[0]
    token_rows = own_hidden.shape[0]
    ulysses_size, cycle_size = 2 * lax.axis_size("chip"), lax.axis_size("blk")
    dp_size = lax.axis_size("dp")
    chip, core = lax.axis_index("chip"), lax.axis_index("core")
    ulysses_index, cycle_index = 2 * chip + core, lax.axis_index("blk")
    dp_index = lax.axis_index("dp")
    block_rows = token_rows * ulysses_size
    span_rows = block_rows // 2
    shard_rows = pair_weight.shape[0]
    kv_width = KVH * HD
    columns = cycle_size * HD

    piece = lax.dynamic_slice(
        pair_weight, (0, core * kv_width + chip * columns), (shard_rows, columns)
    )

    slot_devices = jnp.bitwise_xor(ulysses_index, jnp.arange(ulysses_size, dtype=jnp.int32))
    order_row = span_order[0]
    span_values = lax.dynamic_slice(order_row, (2 * cycle_index,), (2,))
    stored = slot_devices[:, None] * token_rows + jnp.arange(token_rows, dtype=jnp.int32)[None, :]
    stored = stored.reshape(block_rows)
    positions = jnp.where(stored < span_rows, span_values[0], span_values[1]) * span_rows + stored % span_rows
    cosine, sine = wide_tables(positions, yarn_divisor)
    own_cosine, own_sine = cosine[:token_rows], sine[:token_rows]
    pair_cosine = jnp.where(core == 0, cosine, 1.0)
    pair_sine = jnp.where(core == 0, sine, 0.0)

    place = jnp.stack([ulysses_index, cycle_index]).astype(jnp.int32)
    one = jax.ShapeDtypeStruct((token_rows, 2 * HD), jnp.bfloat16)
    by_distance = jax.ShapeDtypeStruct((cycle_size, *one.shape), one.dtype)
    far_queries, *near_queries = pl.pallas_call(
        query_rope_kernel,
        out_shape=[by_distance] + [one] * cycle_size,
        in_specs=[SMEM] + [VMEM] * 3,
        out_specs=[VMEM] * (1 + cycle_size),
        compiler_params=pltpu.CompilerParams(vmem_limit_bytes=8 * 1024 * 1024),
        name="query_rope",
    )(place, queries[0], own_cosine, own_sine)

    def ahead(block, distance=1):
        return lax.ppermute(block, "blk", [(i, (i + distance) % cycle_size) for i in range(cycle_size)])

    def along_blocks(parts):
        moved = {distance: ahead(parts[distance], distance) for distance in far_first(cycle_size)}
        return [moved[distance] for distance in range(1, cycle_size)]

    def across(block):
        return lax.ppermute(block, "dp", [(i, dp_size - 1 - i) for i in range(dp_size)])

    def first_row(distance, row):
        return (row * cycle_size + jnp.remainder(cycle_index - distance, cycle_size)) * shard_rows

    other_row = dp_size - 1 - dp_index
    far = exchange(own_hidden, "chip", 1)
    partner = exchange(own_hidden, "core", 1)

    travelling, crossed = piece, across(piece)
    received = [piece]
    firsts = [first_row(0, dp_index)]
    for distance in range(1, cycle_size):
        firsts += [first_row(distance - 1, other_row), first_row(distance, dp_index)]
    rows = jnp.stack([*firsts, first_row(cycle_size - 1, other_row)])
    for distance in range(1, cycle_size - 1):
        travelling = ahead(travelling)
        if distance == 1:
            far_queries, near_queries, pair_cosine, pair_sine, rows, place, travelling = (
                lax.optimization_barrier(
                    (far_queries, near_queries, pair_cosine, pair_sine, rows, place, travelling)
                )
            )
        travelling, crossed = lax.optimization_barrier((travelling, crossed))
        received += [crossed, travelling]
        crossed = across(travelling)

    far, far_queries, travelling = lax.optimization_barrier((far, far_queries, travelling))
    hidden = [own_hidden, partner, far, exchange(far, "core", 1)]
    far_queries = exchange(far_queries, "chip", 1)
    packed = pl.pallas_call(
        pack_kernel,
        out_shape=[jax.ShapeDtypeStruct((2, *one.shape), one.dtype)] * (cycle_size - 1),
        in_specs=[VMEM] * cycle_size,
        out_specs=[VMEM] * (cycle_size - 1),
        compiler_params=pltpu.CompilerParams(vmem_limit_bytes=8 * 1024 * 1024),
        name="pack",
    )(far_queries, *near_queries[1:])

    travelling = ahead(travelling)
    travelling, crossed, packed = lax.optimization_barrier((travelling, crossed, packed))
    received += [crossed, travelling]
    last_piece = across(travelling)
    packed = along_blocks([None, *packed])
    total, last_hidden = pl.pallas_call(
        functools.partial(terms_kernel, ulysses_size, len(received)),
        out_shape=[
            jax.ShapeDtypeStruct((block_rows, columns), jnp.float32),
            jax.ShapeDtypeStruct((block_rows, shard_rows), jnp.bfloat16),
        ],
        in_specs=[SMEM] + [ANY] * (ulysses_size + len(received)),
        out_specs=[VMEM] * 2,
        scratch_shapes=[
            pltpu.VMEM((len(received), block_rows, shard_rows), jnp.bfloat16),
            pltpu.VMEM((len(received), shard_rows, columns), jnp.bfloat16),
            pltpu.SemaphoreType.DMA((len(received), ulysses_size + 1)),
            pltpu.SemaphoreType.DMA((ulysses_size,)),
        ],
        compiler_params=pltpu.CompilerParams(vmem_limit_bytes=20 * 1024 * 1024),
        name="terms",
    )(rows, *hidden, *received)
    last_piece, total, last_hidden = lax.optimization_barrier((last_piece, total, last_hidden))
    pairs = pl.pallas_call(
        pair_rope_kernel,
        out_shape=[jax.ShapeDtypeStruct((block_rows, HD), jnp.bfloat16)] * cycle_size,
        in_specs=[SMEM] + [VMEM] * 5,
        out_specs=[VMEM] * cycle_size,
        scratch_shapes=[pltpu.VMEM((block_rows, columns), jnp.float32)],
        compiler_params=pltpu.CompilerParams(vmem_limit_bytes=12 * 1024 * 1024),
        name="pair_rope",
    )(place, total, last_hidden, last_piece, pair_cosine, pair_sine)
    pairs, packed = lax.optimization_barrier((pairs, packed))
    mine, theirs = {0: pairs[0]}, {0: exchange(pairs[0], "core", 1)}
    for distance in far_first(cycle_size):
        mine[distance] = ahead(pairs[distance], distance)
        theirs[distance] = exchange(mine[distance], "core", 1)
    in_order = range(cycle_size)

    first = far_first(cycle_size)[0]
    mine[first], packed = lax.optimization_barrier((mine[first], packed))
    sorted_queries = pl.pallas_call(
        sort_queries_kernel,
        out_shape=jax.ShapeDtypeStruct((2 * cycle_size, 2 * token_rows, HD), jnp.bfloat16),
        in_specs=[SMEM, SMEM] + [VMEM] * (1 + cycle_size),
        out_specs=VMEM,
        compiler_params=pltpu.CompilerParams(vmem_limit_bytes=8 * 1024 * 1024),
        name="sort_queries",
    )(span_order, place, near_queries[0], far_queries, *packed)
    sequence_rows = cycle_size * block_rows
    half = jax.ShapeDtypeStruct((cycle_size // 2, *one.shape), one.dtype)
    first_far, last_far, *near = pl.pallas_call(
        attention_kernel,
        out_shape=[half, half] + [one] * cycle_size,
        in_specs=[SMEM, SMEM] + [VMEM] * (1 + 2 * cycle_size),
        out_specs=[VMEM] * (cycle_size + 2),
        scratch_shapes=[
            pltpu.VMEM((sequence_rows, HD), jnp.bfloat16),
            pltpu.VMEM((sequence_rows, HD), jnp.bfloat16),
            pltpu.VMEM((2 * cycle_size, token_rows, 2 * HD), jnp.bfloat16),
        ],
        compiler_params=pltpu.CompilerParams(vmem_limit_bytes=24 * 1024 * 1024),
        name="attention",
    )(
        span_order,
        place,
        sorted_queries,
        *(mine[d] for d in in_order),
        *(theirs[d] for d in in_order),
    )
    halves = [exchange(half, "chip", 1) for half in (first_far, last_far)]
    arrived = [near[0], *along_blocks(near)]
    crossed = {0: halves[1]}
    for index, distance in enumerate(far_first(cycle_size)):
        part, place_in_half = divmod(index, cycle_size // 2)
        crossed[distance] = ahead(halves[part][place_in_half], distance)
    heads = pl.pallas_call(
        order_heads_kernel,
        out_shape=jax.ShapeDtypeStruct((token_rows, QH * HD), jnp.bfloat16),
        in_specs=[SMEM] + [VMEM] * (2 * cycle_size),
        out_specs=VMEM,
        compiler_params=pltpu.CompilerParams(vmem_limit_bytes=8 * 1024 * 1024),
        name="order_heads",
    )(place, *arrived, *(crossed[distance] for distance in in_order))
    return heads[None]


def solution(mesh):
    sizes = dict(mesh.shape)
    specs = dict(
        in_specs=(
            P("dp", ("blk", "ulysses"), None),
            P("dp", ("blk", "ulysses"), None),
            P(("dp", "blk"), None),
            P("dp", None),
            P(),
        ),
        out_specs=P("dp", ("blk", "ulysses"), None),
        check_vma=False,
    )
    whole_cycle = (
        sizes["blk"] == STEPS + 1
        and sizes["ulysses"] == 4
        and sizes["dp"] == 2
        and sizes["ulysses"] * sizes["blk"] == QH == 2 * KVH
    )
    if not whole_cycle:
        return jax.shard_map(general_shards, mesh=mesh, **specs)
    chips = Mesh(
        mesh.devices.reshape(sizes["dp"], sizes["ulysses"] // 2, 2, sizes["blk"]),
        ("dp", "chip", "core", "blk"),
    )
    rows = P("dp", ("blk", "chip", "core"), None)
    specs["in_specs"] = (rows, rows, *specs["in_specs"][2:])
    specs["out_specs"] = rows
    return jax.shard_map(whole_cycle_shards, mesh=chips, **specs)
```

```python
import functools
import math

import jax
import jax.numpy as jnp
from jax import lax
from jax.experimental import pallas as pl
from jax.experimental.pallas import tpu as pltpu
from jax.sharding import Mesh
from jax.sharding import PartitionSpec as P

KVH = 8
HD = 128
QH = 16
STEPS = 3


LOG_BASE = math.log(500000.0)
LOG2_E = math.log2(math.e)


def from_behind(block, axis, distance):
    devices = range(lax.axis_size(axis))
    route = [((i - distance) % len(devices), i) for i in devices]
    return lax.ppermute(block, axis, route)


def rotate(vectors, angle_table):
    half_dim = vectors.shape[-1] // 2
    first_half = vectors[..., :half_dim]
    second_half = vectors[..., half_dim:]
    cosine = jnp.cos(angle_table)
    sine_part = jnp.sin(angle_table)
    return jnp.concatenate(
        [
            first_half * cosine - second_half * sine_part,
            second_half * cosine + first_half * sine_part,
        ],
        axis=-1,
    )


def angles(positions, yarn_divisor):
    half_dim = yarn_divisor.shape[0]
    scaled = 2.0 * jnp.arange(half_dim, dtype=jnp.float32) / (2 * half_dim)
    inverse = jnp.exp(-LOG_BASE * scaled) / yarn_divisor.astype(jnp.float32)
    return positions.astype(jnp.float32)[:, None] * inverse[None, :]


def positions_of(order_row, first_row, row_count, span_rows):
    stored = first_row + jnp.arange(row_count, dtype=jnp.int32)
    span_index = stored // span_rows
    matches = span_index[:, None] == jnp.arange(order_row.shape[0], dtype=jnp.int32)[None, :]
    span_value = jnp.sum(jnp.where(matches, order_row[None, :], 0), axis=1)
    return span_value * span_rows + stored % span_rows


def tile_scores(query_rows, key_rows):
    product = lax.dot_general(
        query_rows, key_rows, (((1,), (1,)), ((), ())), preferred_element_type=jnp.float32
    )
    return product * (1.0 / math.sqrt(HD))


def row_maximum(query_rows, query_pos, key_rows, key_pos):
    score = tile_scores(query_rows, key_rows)
    return jnp.max(jnp.where(key_pos[None, :] <= query_pos[:, None], score, -jnp.inf), axis=1)


def add_tile(denominator, numerator, query_rows, query_pos, key_rows, value_rows, key_pos, row_top):
    score = tile_scores(query_rows, key_rows)
    allowed = key_pos[None, :] <= query_pos[:, None]
    weights = jnp.where(allowed, jnp.exp(score - row_top[:, None]), 0.0)
    denominator = denominator + jnp.sum(weights, axis=1)
    numerator = numerator + jnp.dot(
        weights.astype(jnp.bfloat16), value_rows, preferred_element_type=jnp.float32
    )
    return (denominator, numerator)


def general_shards(hidden_in, queries, pair_weight, span_order, yarn_divisor):
    inputs_local = hidden_in[0]
    queries_local = queries[0]
    order_row = span_order[0]
    token_rows = inputs_local.shape[0]
    ulysses_size = lax.axis_size("ulysses")
    cycle_size = lax.axis_size("blk")
    ulysses_index = lax.axis_index("ulysses")
    cycle_index = lax.axis_index("blk")
    block_rows = token_rows * ulysses_size
    span_rows = block_rows // 2
    kv_width = KVH * HD
    kv_local = KVH // ulysses_size
    group_size = QH // KVH
    own_positions = positions_of(
        order_row, cycle_index * block_rows + ulysses_index * token_rows, token_rows, span_rows
    )
    own_angles = angles(own_positions, yarn_divisor)
    block_positions = positions_of(order_row, cycle_index * block_rows, block_rows, span_rows)
    rotated_queries = rotate(
        queries_local.astype(jnp.float32).reshape(token_rows, QH, HD), own_angles[:, None, :]
    )
    rotated_queries = rotated_queries.astype(jnp.bfloat16).reshape(token_rows, QH * HD)
    projected = jnp.dot(
        inputs_local,
        lax.all_gather(pair_weight, ("dp", "blk"), axis=0, tiled=True),
        preferred_element_type=jnp.float32,
    )
    token_keys = rotate(
        projected[:, :kv_width].reshape(token_rows, KVH, HD), own_angles[:, None, :]
    )
    token_keys = token_keys.astype(jnp.bfloat16).reshape(token_rows, kv_width)
    token_values = projected[:, kv_width:].astype(jnp.bfloat16)
    query_block, key_block, value_block = (
        lax.all_to_all(rotated_queries, "ulysses", split_axis=1, concat_axis=0, tiled=True),
        lax.all_to_all(token_keys, "ulysses", split_axis=1, concat_axis=0, tiled=True),
        lax.all_to_all(token_values, "ulysses", split_axis=1, concat_axis=0, tiled=True),
    )
    own_pair = jnp.stack([key_block, value_block])
    carried_blocks = [own_pair]
    current_pair = own_pair
    for step_index in range(STEPS):
        current_pair = from_behind(current_pair, "blk", 1)
        carried_blocks.append(current_pair)
    carried_positions = []
    for step_index in range(STEPS + 1):
        source_block = jnp.remainder(cycle_index - step_index, cycle_size)
        carried_positions.append(
            positions_of(order_row, source_block * block_rows, block_rows, span_rows)
        )
    output_rows = []
    for query_half in range(2):
        row_start = query_half * span_rows
        half_positions = block_positions[row_start : row_start + span_rows]
        query_pos = jnp.tile(half_positions, group_size)
        head_outputs = []
        for local_head in range(kv_local):
            query_part = query_block[
                row_start : row_start + span_rows,
                local_head * group_size * HD : (local_head + 1) * group_size * HD,
            ]
            query_rows = (
                query_part.reshape(span_rows, group_size, HD)
                .transpose(1, 0, 2)
                .reshape(group_size * span_rows, HD)
            )
            tile_list = []
            for step_index in range(STEPS + 1):
                pair_block = carried_blocks[step_index]
                for key_half in range(2):
                    key_start = key_half * span_rows
                    key_rows = pair_block[
                        0,
                        key_start : key_start + span_rows,
                        local_head * HD : (local_head + 1) * HD,
                    ]
                    value_rows = pair_block[
                        1,
                        key_start : key_start + span_rows,
                        local_head * HD : (local_head + 1) * HD,
                    ]
                    key_pos = carried_positions[step_index][key_start : key_start + span_rows]
                    tile_list.append((key_rows, value_rows, key_pos))
            row_top = jnp.full((group_size * span_rows,), -jnp.inf, jnp.float32)
            for key_rows, value_rows, key_pos in tile_list:
                tile_top = row_maximum(query_rows, query_pos, key_rows, key_pos)
                row_top = jnp.maximum(row_top, tile_top)
            denominator = jnp.zeros((group_size * span_rows,), jnp.float32)
            numerator = jnp.zeros((group_size * span_rows, HD), jnp.float32)
            for key_rows, value_rows, key_pos in tile_list:
                denominator, numerator = add_tile(
                    denominator,
                    numerator,
                    query_rows,
                    query_pos,
                    key_rows,
                    value_rows,
                    key_pos,
                    row_top,
                )
            normalized = (numerator / denominator[:, None]).astype(jnp.bfloat16)
            normalized = (
                normalized.reshape(group_size, span_rows, HD)
                .transpose(1, 0, 2)
                .reshape(span_rows, group_size * HD)
            )
            head_outputs.append(normalized)
        output_rows.append(jnp.concatenate(head_outputs, axis=1))
    block_output = jnp.concatenate(output_rows, axis=0)
    token_output = lax.all_to_all(block_output, "ulysses", split_axis=0, concat_axis=1, tiled=True)
    return token_output[None]


def far_first(size):
    return sorted(range(1, size), key=lambda distance: -min(distance, size - distance))


def exchange(block, axis, distance):
    size = lax.axis_size(axis)
    return lax.ppermute(block, axis, [(i, i ^ distance) for i in range(size)])


def wide_tables(positions, yarn_divisor):
    angle_table = angles(positions, yarn_divisor)
    cosine, sine = jnp.cos(angle_table), jnp.sin(angle_table)
    return jnp.concatenate([cosine, cosine], axis=1), jnp.concatenate([-sine, sine], axis=1)


def rope_head(head, cosine, signed_sine):
    return head * cosine + pltpu.roll(head, HD // 2, 1) * signed_sine


def query_rope_kernel(place_ref, query_ref, cosine_ref, sine_ref, far_ref, *near_refs):
    cosine, sine = cosine_ref[...], sine_ref[...]
    blocks, width = far_ref.shape[0], far_ref.shape[2]
    chip, block_here = place_ref[0] // 2, place_ref[1]
    for distance, near_ref in enumerate(near_refs):
        block = lax.rem(block_here + distance, blocks)
        for target, out_ref in ((chip, near_ref), (1 - chip, far_ref.at[distance])):
            columns = pl.ds(pl.multiple_of((target * blocks + block) * width, width), width)
            pair = query_ref[:, columns].astype(jnp.float32)
            for start in range(0, width, HD):
                rows = rope_head(pair[:, start : start + HD], cosine, sine)
                out_ref[:, start : start + HD] = rows.astype(jnp.bfloat16)


def pack_kernel(far_ref, *refs):
    near_refs, out_refs = refs[: len(refs) // 2], refs[len(refs) // 2 :]
    for distance, (near_ref, out_ref) in enumerate(zip(near_refs, out_refs), 1):
        out_ref[0] = near_ref[...]
        out_ref[1] = far_ref[distance]


def load_terms(rows_ref, slot_refs, piece_refs, hidden_rows, pieces, sems):
    token_rows = slot_refs[0].shape[0]
    copies = []
    for index, piece_ref in enumerate(piece_refs):
        depth = piece_ref.shape[0]
        columns = pl.ds(pl.multiple_of(rows_ref[index], depth), depth)
        started = [pltpu.make_async_copy(piece_ref, pieces.at[index], sems.at[index, 0])]
        for slot, slot_ref in enumerate(slot_refs):
            rows = hidden_rows.at[index, pl.ds(slot * token_rows, token_rows)]
            started.append(pltpu.make_async_copy(slot_ref.at[:, columns], rows, sems.at[index, slot + 1]))
        for copy in started:
            copy.start()
        copies.append(started)
    return copies


def terms_kernel(slots, count, rows_ref, *refs):
    slot_refs, piece_refs = refs[:slots], refs[slots : slots + count]
    out_ref, next_hidden_ref, hidden_rows, pieces, sems, next_sems = refs[slots + count :]
    copies = load_terms(rows_ref, slot_refs, piece_refs, hidden_rows, pieces, sems)
    token_rows, depth = slot_refs[0].shape[0], piece_refs[0].shape[0]
    columns = pl.ds(pl.multiple_of(rows_ref[count], depth), depth)
    next_copies = [
        pltpu.make_async_copy(
            slot_ref.at[:, columns],
            next_hidden_ref.at[pl.ds(slot * token_rows, token_rows)],
            next_sems.at[slot],
        )
        for slot, slot_ref in enumerate(slot_refs)
    ]
    for copy in next_copies:
        copy.start()
    total = None
    for index, started in enumerate(copies):
        for copy in started:
            copy.wait()
        term = jnp.dot(hidden_rows[index], pieces[index], preferred_element_type=jnp.float32)
        total = term if total is None else total + term
    out_ref[...] = total
    for copy in next_copies:
        copy.wait()


def pair_rope_kernel(place_ref, total_ref, hidden_ref, piece_ref, cosine_ref, sine_ref, *refs):
    out_refs, sum_ref = refs[:-1], refs[-1]
    sum_ref[...] = total_ref[...] + jnp.dot(
        hidden_ref[...], piece_ref[...], preferred_element_type=jnp.float32
    )
    cosine, sine = cosine_ref[...], sine_ref[...]
    for distance, out_ref in enumerate(out_refs):
        head = lax.rem(place_ref[1] + distance, len(out_refs))
        rows = sum_ref[:, pl.ds(pl.multiple_of(head * HD, HD), HD)]
        out_ref[...] = rope_head(rows, cosine, sine).astype(jnp.bfloat16)


def place_heads_kernel(crossed, distances, place_ref, *refs):
    out_ref, sems = refs[-2:]
    blocks, chip, block_here = out_ref.shape[1] // (4 * HD), place_ref[0] // 2, place_ref[1]
    width = 2 * HD
    copies = []
    for index, (distance, rows) in enumerate(zip(distances, refs)):
        block = lax.rem(block_here + blocks - distance, blocks)
        source = 1 - chip if crossed[index] else chip
        columns = pl.ds(pl.multiple_of((source * blocks + block) * width, width), width)
        rows = rows.at[rows.shape[0] - 1] if len(rows.shape) == 3 else rows
        copies.append(pltpu.make_async_copy(rows, out_ref.at[:, columns], sems.at[index]))
        copies[-1].start()
    for copy in copies:
        copy.wait()


def attention_kernel(order_ref, place_ref, *refs):
    spans = order_ref.shape[1]
    blocks = spans // 2
    mine_refs, theirs_refs = refs[:blocks], refs[blocks : 2 * blocks]
    near_query, far_query, *packed_queries = refs[2 * blocks : 3 * blocks + 1]
    first_far_ref, last_far_ref, *near_refs = refs[3 * blocks + 1 : -4]
    key_rows, value_rows, query_rows, out_rows = refs[-4:]
    token_rows = query_rows.shape[1]
    span_rows = 2 * token_rows
    place, block_here = place_ref[0], place_ref[1]
    chip, core = place // 2, place % 2
    for distance in range(blocks):
        block = lax.rem(block_here + blocks - distance, blocks)
        packed = packed_queries[distance - 1] if distance else None
        query_rows[2 * block + chip] = packed[0] if distance else near_query[...]
        query_rows[2 * block + 1 - chip] = packed[1] if distance else far_query[0]
        for half in range(2):
            first = order_ref[0, 2 * block + half] * span_rows
            for part in range(2):
                slot = jnp.bitwise_xor(half * 2 + part, place)
                other = jnp.bitwise_xor(slot, 1)
                mine = mine_refs[distance][pl.ds(pl.multiple_of(slot * token_rows, token_rows), token_rows), :]
                theirs = theirs_refs[distance][
                    pl.ds(pl.multiple_of(other * token_rows, token_rows), token_rows), :
                ]
                rows = pl.ds(pl.multiple_of(first + part * token_rows, token_rows), token_rows)
                key_rows[rows, :] = jnp.where(core == 0, mine, theirs)
                value_rows[rows, :] = jnp.where(core == 0, theirs, mine)
    stored = []
    for position in range(spans):
        span = jnp.int32(0)
        for candidate in range(1, spans):
            span = jnp.where(order_ref[0, candidate] == position, candidate, span)
        stored.append(span)
    square = (2 * token_rows, span_rows)
    row_index = lax.broadcasted_iota(jnp.int32, square, 0) % token_rows + core * token_rows
    allowed = lax.broadcasted_iota(jnp.int32, square, 1) <= row_index

    def scores(position):
        pair = query_rows[stored[position]]
        query = jnp.concatenate([pair[:, :HD], pair[:, HD:]], axis=0)
        score = lax.dot_general(
            query,
            key_rows[: (position + 1) * span_rows, :],
            (((1,), (1,)), ((), ())),
            preferred_element_type=jnp.float32,
        )
        start = position * span_rows
        last = jnp.where(allowed, score[:, start:], -jnp.inf)
        return jnp.concatenate([score[:, :start], last], axis=1) if position else last

    score = scores(spans - 1)
    for position in reversed(range(spans)):
        following = scores(position - 1) if position else None
        row_top = jnp.max(score, axis=1, keepdims=True)
        weights = jnp.exp2((score - row_top) * (LOG2_E / math.sqrt(HD)))
        denominator = jnp.sum(weights, axis=1, keepdims=True)
        numerator = jnp.dot(
            weights.astype(jnp.bfloat16),
            value_rows[: (position + 1) * span_rows, :],
            preferred_element_type=jnp.float32,
        )
        rows = (numerator / denominator).astype(jnp.bfloat16)
        out_rows[stored[position]] = jnp.concatenate([rows[:token_rows], rows[token_rows:]], axis=1)
        score = following
    for distance, near_ref in enumerate(near_refs):
        block = lax.rem(block_here + distance, blocks)
        near_ref[...] = out_rows[2 * block + chip]
    order = [*far_first(blocks), 0]
    for index, distance in enumerate(order):
        block = lax.rem(block_here + distance, blocks)
        half, place_in_half = divmod(index, blocks // 2)
        (first_far_ref, last_far_ref)[half][place_in_half] = out_rows[2 * block + 1 - chip]


VMEM = pl.BlockSpec(memory_space=pltpu.VMEM)
ANY = pl.BlockSpec(memory_space=pl.ANY)
SMEM = pl.BlockSpec(memory_space=pltpu.SMEM)


def whole_cycle_shards(hidden_in, queries, pair_weight, span_order, yarn_divisor):
    own_hidden = hidden_in[0]
    token_rows = own_hidden.shape[0]
    ulysses_size, cycle_size = 2 * lax.axis_size("chip"), lax.axis_size("blk")
    dp_size = lax.axis_size("dp")
    chip, core = lax.axis_index("chip"), lax.axis_index("core")
    ulysses_index, cycle_index = 2 * chip + core, lax.axis_index("blk")
    dp_index = lax.axis_index("dp")
    block_rows = token_rows * ulysses_size
    span_rows = block_rows // 2
    shard_rows = pair_weight.shape[0]
    kv_width = KVH * HD
    columns = cycle_size * HD

    piece = lax.dynamic_slice(
        pair_weight, (0, core * kv_width + chip * columns), (shard_rows, columns)
    )

    slot_devices = jnp.bitwise_xor(ulysses_index, jnp.arange(ulysses_size, dtype=jnp.int32))
    order_row = span_order[0]
    span_values = lax.dynamic_slice(order_row, (2 * cycle_index,), (2,))
    stored = slot_devices[:, None] * token_rows + jnp.arange(token_rows, dtype=jnp.int32)[None, :]
    stored = stored.reshape(block_rows)
    positions = jnp.where(stored < span_rows, span_values[0], span_values[1]) * span_rows + stored % span_rows
    cosine, sine = wide_tables(positions, yarn_divisor)
    own_cosine, own_sine = cosine[:token_rows], sine[:token_rows]
    pair_cosine = jnp.where(core == 0, cosine, 1.0)
    pair_sine = jnp.where(core == 0, sine, 0.0)

    place = jnp.stack([ulysses_index, cycle_index]).astype(jnp.int32)
    one = jax.ShapeDtypeStruct((token_rows, 2 * HD), jnp.bfloat16)
    by_distance = jax.ShapeDtypeStruct((cycle_size, *one.shape), one.dtype)
    far_queries, *near_queries = pl.pallas_call(
        query_rope_kernel,
        out_shape=[by_distance] + [one] * cycle_size,
        in_specs=[SMEM] + [VMEM] * 3,
        out_specs=[VMEM] * (1 + cycle_size),
        compiler_params=pltpu.CompilerParams(vmem_limit_bytes=8 * 1024 * 1024),
        name="query_rope",
    )(place, queries[0], own_cosine, own_sine)

    def ahead(block, distance=1):
        return lax.ppermute(block, "blk", [(i, (i + distance) % cycle_size) for i in range(cycle_size)])

    def along_blocks(parts):
        moved = {distance: ahead(parts[distance], distance) for distance in far_first(cycle_size)}
        return [moved[distance] for distance in range(1, cycle_size)]

    def across(block):
        return lax.ppermute(block, "dp", [(i, dp_size - 1 - i) for i in range(dp_size)])

    def first_row(distance, row):
        return (row * cycle_size + jnp.remainder(cycle_index - distance, cycle_size)) * shard_rows

    other_row = dp_size - 1 - dp_index
    far = exchange(own_hidden, "chip", 1)
    partner = exchange(own_hidden, "core", 1)

    travelling, crossed = piece, across(piece)
    received = [piece]
    firsts = [first_row(0, dp_index)]
    for distance in range(1, cycle_size):
        firsts += [first_row(distance - 1, other_row), first_row(distance, dp_index)]
    rows = jnp.stack([*firsts, first_row(cycle_size - 1, other_row)])
    for distance in range(1, cycle_size - 1):
        travelling = ahead(travelling)
        if distance == 1:
            far_queries, near_queries, pair_cosine, pair_sine, rows, place, travelling = (
                lax.optimization_barrier(
                    (far_queries, near_queries, pair_cosine, pair_sine, rows, place, travelling)
                )
            )
        travelling, crossed = lax.optimization_barrier((travelling, crossed))
        received += [crossed, travelling]
        crossed = across(travelling)

    far, far_queries, travelling = lax.optimization_barrier((far, far_queries, travelling))
    hidden = [own_hidden, partner, far, exchange(far, "core", 1)]
    far_queries = exchange(far_queries, "chip", 1)
    packed = pl.pallas_call(
        pack_kernel,
        out_shape=[jax.ShapeDtypeStruct((2, *one.shape), one.dtype)] * (cycle_size - 1),
        in_specs=[VMEM] * cycle_size,
        out_specs=[VMEM] * (cycle_size - 1),
        compiler_params=pltpu.CompilerParams(vmem_limit_bytes=8 * 1024 * 1024),
        name="pack",
    )(far_queries, *near_queries[1:])

    travelling = ahead(travelling)
    travelling, crossed, packed = lax.optimization_barrier((travelling, crossed, packed))
    received += [crossed, travelling]
    last_piece = across(travelling)
    packed = along_blocks([None, *packed])
    total, last_hidden = pl.pallas_call(
        functools.partial(terms_kernel, ulysses_size, len(received)),
        out_shape=[
            jax.ShapeDtypeStruct((block_rows, columns), jnp.float32),
            jax.ShapeDtypeStruct((block_rows, shard_rows), jnp.bfloat16),
        ],
        in_specs=[SMEM] + [ANY] * (ulysses_size + len(received)),
        out_specs=[VMEM] * 2,
        scratch_shapes=[
            pltpu.VMEM((len(received), block_rows, shard_rows), jnp.bfloat16),
            pltpu.VMEM((len(received), shard_rows, columns), jnp.bfloat16),
            pltpu.SemaphoreType.DMA((len(received), ulysses_size + 1)),
            pltpu.SemaphoreType.DMA((ulysses_size,)),
        ],
        compiler_params=pltpu.CompilerParams(vmem_limit_bytes=20 * 1024 * 1024),
        name="terms",
    )(rows, *hidden, *received)
    last_piece, total, last_hidden = lax.optimization_barrier((last_piece, total, last_hidden))
    pairs = pl.pallas_call(
        pair_rope_kernel,
        out_shape=[jax.ShapeDtypeStruct((block_rows, HD), jnp.bfloat16)] * cycle_size,
        in_specs=[SMEM] + [VMEM] * 5,
        out_specs=[VMEM] * cycle_size,
        scratch_shapes=[pltpu.VMEM((block_rows, columns), jnp.float32)],
        compiler_params=pltpu.CompilerParams(vmem_limit_bytes=12 * 1024 * 1024),
        name="pair_rope",
    )(place, total, last_hidden, last_piece, pair_cosine, pair_sine)
    pairs, packed = lax.optimization_barrier((pairs, packed))
    mine, theirs = {0: pairs[0]}, {0: exchange(pairs[0], "core", 1)}
    for distance in far_first(cycle_size):
        mine[distance] = ahead(pairs[distance], distance)
        theirs[distance] = exchange(mine[distance], "core", 1)
    in_order = range(cycle_size)

    sequence_rows = cycle_size * block_rows
    half = jax.ShapeDtypeStruct((cycle_size // 2, *one.shape), one.dtype)
    first_far, last_far, *near = pl.pallas_call(
        attention_kernel,
        out_shape=[half, half] + [one] * cycle_size,
        in_specs=[SMEM, SMEM] + [VMEM] * (3 * cycle_size + 1),
        out_specs=[VMEM] * (cycle_size + 2),
        scratch_shapes=[
            pltpu.VMEM((sequence_rows, HD), jnp.bfloat16),
            pltpu.VMEM((sequence_rows, HD), jnp.bfloat16),
            pltpu.VMEM((2 * cycle_size, token_rows, 2 * HD), jnp.bfloat16),
            pltpu.VMEM((2 * cycle_size, token_rows, 2 * HD), jnp.bfloat16),
        ],
        compiler_params=pltpu.CompilerParams(vmem_limit_bytes=24 * 1024 * 1024),
        name="attention",
    )(
        span_order,
        place,
        *(mine[d] for d in in_order),
        *(theirs[d] for d in in_order),
        near_queries[0],
        far_queries,
        *packed,
    )
    halves = [exchange(half, "chip", 1) for half in (first_far, last_far)]
    arrived = [near[0], *along_blocks(near)]
    crossed = {0: halves[1]}
    for index, distance in enumerate(far_first(cycle_size)):
        part, place_in_half = divmod(index, cycle_size // 2)
        crossed[distance] = ahead(halves[part][place_in_half], distance)
    def place_heads(crossed, distances, parts, before):
        extra = [] if before is None else [before]
        return pl.pallas_call(
            functools.partial(place_heads_kernel, crossed, distances),
            out_shape=jax.ShapeDtypeStruct((token_rows, QH * HD), jnp.bfloat16),
            in_specs=[SMEM] + [VMEM] * len(parts) + [ANY] * len(extra),
            out_specs=ANY,
            scratch_shapes=[pltpu.SemaphoreType.DMA((len(parts),))],
            input_output_aliases={1 + len(parts): 0} if extra else {},
            compiler_params=pltpu.CompilerParams(vmem_limit_bytes=8 * 1024 * 1024),
            name="place_heads",
        )(place, *parts, *extra)

    early = [*in_order, 0]
    heads = place_heads(
        [False] * cycle_size + [True], early, [*(arrived[d] for d in in_order), crossed[0]], None
    )
    late = list(in_order)[1:]
    heads = place_heads([True] * len(late), late, [crossed[d] for d in late], heads)
    return heads[None]


def solution(mesh):
    sizes = dict(mesh.shape)
    specs = dict(
        in_specs=(
            P("dp", ("blk", "ulysses"), None),
            P("dp", ("blk", "ulysses"), None),
            P(("dp", "blk"), None),
            P("dp", None),
            P(),
        ),
        out_specs=P("dp", ("blk", "ulysses"), None),
        check_vma=False,
    )
    whole_cycle = (
        sizes["blk"] == STEPS + 1
        and sizes["ulysses"] == 4
        and sizes["dp"] == 2
        and sizes["ulysses"] * sizes["blk"] == QH == 2 * KVH
    )
    if not whole_cycle:
        return jax.shard_map(general_shards, mesh=mesh, **specs)
    chips = Mesh(
        mesh.devices.reshape(sizes["dp"], sizes["ulysses"] // 2, 2, sizes["blk"]),
        ("dp", "chip", "core", "blk"),
    )
    rows = P("dp", ("blk", "chip", "core"), None)
    specs["in_specs"] = (rows, rows, *specs["in_specs"][2:])
    specs["out_specs"] = rows
    return jax.shard_map(whole_cycle_shards, mesh=chips, **specs)
```
